128 devices in a mesh: dp: 16 (over x, y_lo, core), tensor: 8 (over y_hi, z).
Axes of the slice: x: 4, y: 4 (y_hi: 2, y_lo: 2; y = y_hi * 2 + y_lo), z: 4, core: 2. Of those that a mesh axis runs over, the one named last changes fastest.
Arguments:
- block_input: float32 [16384, 2048], P(('dp', 'tensor')), may hold values from -6 to 6
- segments: int32 [16384], P('dp'), may hold values from 0 to 63, as said below
- positions: int32 [16384], P('dp'), may hold values from 0 to 1086, as said below
- attn_gain: float32 [2048], replicated, may hold values from 0.5 to 1.5
- w_query: bfloat16 [2048, 2048], P('dp', 'tensor'), may hold values from -0.125 to 0.125
- w_key: bfloat16 [2048, 2048], P('dp', 'tensor'), may hold values from -0.125 to 0.125
- w_value: bfloat16 [2048, 2048], P('dp', 'tensor'), may hold values from -0.125 to 0.125
- w_output: bfloat16 [2048, 2048], P('tensor', 'dp'), may hold values from -2 to 2
- mlp_gain: float32 [2048], replicated, may hold values from 0.5 to 1.5
- w_gate: bfloat16 [2048, 5504], P('dp', 'tensor'), may hold values from -0.125 to 0.125
- w_up: bfloat16 [2048, 5504], P('dp', 'tensor'), may hold values from -0.125 to 0.125
- w_down: bfloat16 [5504, 2048], P('tensor', 'dp'), may hold values from -0.078125 to 0.078125
- cotangent: float32 [16384, 2048], P(('dp', 'tensor')), may hold values from -24 to 24
Outputs:
- out_block: float32 [16384, 2048], P(('dp', 'tensor'))
- grad_input: float32 [16384, 2048], P(('dp', 'tensor'))
- grad_attn_gain: float32 [2048], replicated
- grad_query: float32 [2048, 2048], P('dp', 'tensor')
- grad_key: float32 [2048, 2048], P('dp', 'tensor')
- grad_value: float32 [2048, 2048], P('dp', 'tensor')
- grad_output: float32 [2048, 2048], P('tensor', 'dp')
- grad_mlp_gain: float32 [2048], replicated
- grad_gate: float32 [2048, 5504], P('dp', 'tensor')
- grad_up: float32 [2048, 5504], P('dp', 'tensor')
- grad_down: float32 [5504, 2048], P('tensor', 'dp')
The draws below stay inside these ranges and needn't reach their ends.
Inputs may be any that keep to these rules, and one draw needn't show every extreme that they name: `segments`: each sequence of 1024 tokens holds four documents in order, numbered 4 * (the sequence's index) + 0, 1, 2, 3; the first has at most 64 tokens and the last two together at most 65. `positions`: positions rise by one from token to token within a document; documents 1 to 3 of a sequence start at 0, the first may continue one begun earlier and start higher.
All inputs are finite; a program needn't handle non-finite values.
Results may differ from the reference program's by a relative error of at most 0.022.
Values may be sent and summed in bfloat16 or wider, within the bound.
No kernel may reach another device: no remote copies, remote signals or barrier semaphores. Data moves between devices by JAX's collectives and lax.ppermute only.
A program may use at most 128 MiB of HBM per device.

```python
import jax
import jax.numpy as jnp
from jax import lax

D = 2048
HEADS = 16
HEAD_DIM = 128
FF = 5504
LEN = 1024
TOKENS = 16384


def document_layout(key):
    seq_count = TOKENS // LEN
    head_key, tail_key, last_key, pick_key = jax.random.split(key, 4)
    head_len = jax.random.randint(head_key, (seq_count, 1), 1, LEN // 16 + 1)
    chosen_seq = jax.random.randint(pick_key, (), 0, seq_count)
    chosen = jnp.arange(seq_count, dtype=jnp.int32)[:, None] == chosen_seq
    head_len = jnp.where(chosen, LEN // 16, head_len)
    tail_len = jax.random.randint(tail_key, (seq_count, 1), 2, LEN // 16 + 2)
    last_len = jax.random.randint(last_key, (seq_count, 1), 1, tail_len)
    token_index = jnp.arange(LEN, dtype=jnp.int32)[None, :]
    second_start = head_len
    third_start = LEN - tail_len
    fourth_start = LEN - last_len
    doc_number = (token_index >= second_start).astype(jnp.int32) + (token_index >= third_start).astype(jnp.int32) + (token_index >= fourth_start).astype(jnp.int32)
    return (doc_number, token_index, second_start, third_start, fourth_start, chosen)


def draw_segments(key, part):
    doc_number, token_index, second_start, third_start, fourth_start, chosen = document_layout(key)
    seq_base = 4 * jnp.arange(TOKENS // LEN, dtype=jnp.int32)[:, None]
    return (doc_number + seq_base).reshape(TOKENS)


def draw_positions(key, part):
    doc_number, token_index, second_start, third_start, fourth_start, chosen = document_layout(key)
    key = jax.random.fold_in(key, 5)
    carried = jax.random.randint(key, (TOKENS // LEN, 1), 0, LEN)
    carried = jnp.where(chosen, LEN - 1, carried)
    doc_start = jnp.where(doc_number == 0, -carried, jnp.where(doc_number == 1, second_start, jnp.where(doc_number == 2, third_start, fourth_start)))
    return (token_index - doc_start).reshape(TOKENS)


def strengthened(entries, own_key, source, target, blocks, factor):
    owner, partner = [(jnp.arange(entries.shape[position]) // (entries.shape[position] // blocks)).reshape([-1 if axis == position else 1 for axis in range(entries.ndim)]) for position in (source, target)]
    chosen = jax.random.permutation(own_key, blocks)[partner]
    strong = (owner == chosen) | (owner == (partner + blocks // 2) % blocks)
    return jnp.where(strong, factor * entries, entries)


def shard_levels(rng, extent, shards, low, top_value):
    def one(dim, parts):
        steps = jax.random.uniform(jax.random.fold_in(jax.random.fold_in(rng, 6), dim), (parts,), jnp.float32, low / len(shards), top_value / len(shards))
        return jnp.repeat(jnp.exp(steps), extent[dim] // parts).reshape((-1,) + (1,) * (len(extent) - dim - 1))

    gain = one(*shards[0])
    for cut in shards[1:]:
        gain = gain * one(*cut)
    return gain


def bell_draw(key, extent, deviation, reach, cuts=(), kind=jnp.bfloat16):
    drawn = deviation * jax.random.normal(key, extent, jnp.float32)
    if cuts:
        drawn = drawn * shard_levels(key, extent, cuts, -0.22, 0.18)
    return jnp.clip(drawn, -reach, reach).astype(kind)


def gaussian_with(stream_key, extent, deviation, bound, shards, heavy, kind=jnp.bfloat16):
    array = deviation * jax.random.normal(stream_key, extent, jnp.float32)
    if shards:
        array = array * shard_levels(stream_key, extent, shards, -0.22, 0.18)
    return jnp.clip(strengthened(array, jax.random.fold_in(stream_key, 3), *heavy), -bound, bound).astype(kind)


def setup_inputs(seed: int = 0) -> dict:
    splits = jax.random.split(jax.random.key(seed), 14)
    return {
        "block_input": bell_draw(splits[0], (TOKENS, D), 1.0, 6.0, ((0, 128),), jnp.float32),
        "segments": draw_segments(jax.random.fold_in(splits[13], 71), 0),
        "positions": draw_positions(jax.random.fold_in(splits[13], 71), 0),
        "attn_gain": jnp.clip(1.0 + 0.1 * jax.random.normal(splits[3], (D,), jnp.float32), 0.5, 1.5),
        "w_query": bell_draw(splits[4], (D, D), D ** -0.5, 0.125, ((0, 16), (1, 8))),
        "w_key": bell_draw(splits[5], (D, D), D ** -0.5, 0.125, ((0, 16), (1, 8))),
        "w_value": bell_draw(splits[6], (D, D), D ** -0.5, 0.125, ((0, 16), (1, 8))),
        "w_output": bell_draw(splits[7], (D, D), (max(1, 4 * D // LEN)) ** -0.5, 2.0, ((0, 8), (1, 16))),
        "mlp_gain": jnp.clip(1.0 + 0.1 * jax.random.normal(splits[8], (D,), jnp.float32), 0.5, 1.5),
        "w_gate": bell_draw(splits[9], (D, FF), D ** -0.5, 0.125, ((0, 16), (1, 8))),
        "w_up": bell_draw(splits[10], (D, FF), D ** -0.5, 0.125, ((0, 16), (1, 8))),
        "w_down": bell_draw(splits[11], (FF, D), FF ** -0.5, 0.078125, ((0, 8), (1, 16))),
        "cotangent": gaussian_with(splits[12], (TOKENS, D), 1.0, 24.0, ((0, 128),), (0, 1, 128, 5.5), jnp.float32),
    }


@jax.custom_vjp
def low(v):
    return lax.optimization_barrier(v.astype(jnp.bfloat16)).astype(jnp.float32)

@jax.custom_vjp
def low_back(v):
    return v

def low_keep(v):
    return (low(v), None)

def low_pass(kept, grad):
    return (grad,)

def back_keep(v):
    return (v, None)

def back_low(kept, grad):
    return (low(grad),)
low.defvjp(low_keep, low_pass)
low_back.defvjp(back_keep, back_low)
epsilon = 1e-05
base_freq = 10000.0
highest = lax.Precision.HIGHEST

def matmul(left, right):
    return jnp.dot(left, right, precision=highest, preferred_element_type=jnp.float32)

def rms_norm(stream, gain_vector):
    return stream * lax.rsqrt(lax.optimization_barrier(jnp.mean(stream * stream, axis=-1, keepdims=True)) + epsilon) * gain_vector

def rotary_tables(token_positions):
    half_dim = HEAD_DIM // 2
    frequency = base_freq ** (-(2.0 * jnp.arange(half_dim, dtype=jnp.float32)) / HEAD_DIM)
    angles = token_positions.astype(jnp.float32)[:, None] * frequency[None, :]
    return (jnp.cos(angles)[:, None, :], jnp.sin(angles)[:, None, :])

def rotate(vectors, cosine, sine_table):
    first_half, second_half = jnp.split(vectors, 2, axis=-1)
    return jnp.concatenate([first_half * cosine - second_half * sine_table, second_half * cosine + first_half * sine_table], axis=-1)

def attend_block(query_block, first_row, key_rows, value_rows, seg_seq):
    block_rows = query_block.shape[0]
    logits = jnp.einsum('qhd,khd->hqk', query_block, key_rows, precision=highest, preferred_element_type=jnp.float32) * HEAD_DIM ** (-0.5)
    logits = low_back(logits)
    query_index = first_row + jnp.arange(block_rows, dtype=jnp.int32)
    key_index = jnp.arange(seg_seq.shape[0], dtype=jnp.int32)
    query_seg = lax.dynamic_slice_in_dim(seg_seq, first_row, block_rows, 0)
    allowed = (query_seg[:, None] == seg_seq[None, :]) & (key_index[None, :] <= query_index[:, None])
    masked = jnp.where(allowed[None], logits, -1e+30)
    row_max = lax.optimization_barrier(jnp.max(masked, axis=-1, keepdims=True))
    exponent = jnp.exp(masked - row_max)
    softmax_rows = exponent / lax.optimization_barrier(jnp.sum(exponent, axis=-1, keepdims=True))
    return jnp.einsum('hqk,khd->qhd', low(softmax_rows), value_rows, precision=highest, preferred_element_type=jnp.float32)

def attend(queries, key_rows, value_rows, seg_seq):
    block_rows = min(512, LEN)
    block_count = LEN // block_rows
    blocks = queries.reshape(block_count, block_rows, HEADS, HEAD_DIM)
    starts = jnp.arange(block_count, dtype=jnp.int32) * block_rows

    def one_block(inputs):
        return attend_block(inputs[0], inputs[1], key_rows, value_rows, seg_seq)
    outputs = lax.map(jax.checkpoint(one_block), (blocks, starts))
    return outputs.reshape(LEN, HEADS, HEAD_DIM)

def layer(params, stream, seg_seq, cosine, sine_table):
    attn_gain, w_query, w_key, w_value, w_output, mlp_gain, w_gate, w_up, w_down = params
    shape_heads = (LEN, HEADS, HEAD_DIM)
    act_first = low(rms_norm(stream, attn_gain))
    queries = low(rotate(low_back(matmul(act_first, w_query)).reshape(shape_heads), cosine, sine_table))
    key_rows = low(rotate(low_back(matmul(act_first, w_key)).reshape(shape_heads), cosine, sine_table))
    value_rows = low(low_back(matmul(act_first, w_value))).reshape(shape_heads)
    attended = low(low_back(attend(queries, key_rows, value_rows, seg_seq).reshape(LEN, D)))
    middle = stream + low_back(matmul(attended, w_output))
    act_second = low(rms_norm(middle, mlp_gain))
    gate_value = low_back(matmul(act_second, w_gate))
    up_value = low_back(matmul(act_second, w_up))
    hidden = low(jax.nn.silu(gate_value) * up_value)
    return middle + low_back(matmul(hidden, w_down))

def reference(block_input, segments, positions, attn_gain, w_query, w_key, w_value, w_output, mlp_gain, w_gate, w_up, w_down, cotangent):
    params = tuple((p.astype(jnp.float32) for p in (attn_gain, w_query, w_key, w_value, w_output, mlp_gain, w_gate, w_up, w_down)))
    seq_count = TOKENS // LEN
    streams = block_input.astype(jnp.float32).reshape(seq_count, LEN, D)
    grads_in = cotangent.astype(jnp.float32).reshape(seq_count, LEN, D)
    seg_all = segments.reshape(seq_count, LEN)
    pos_all = positions.reshape(seq_count, LEN)

    def one_sequence(running, inputs):
        stream, gradient, seg_seq, pos_seq = inputs
        cosine, sine_table = rotary_tables(pos_seq)

        def forward(weights, values):
            return layer(weights, values, seg_seq, cosine, sine_table)
        result, pullback = jax.vjp(forward, params, stream)
        weight_grads, stream_grad = pullback(gradient)
        running = jax.tree.map(lambda a, b: a + b, running, weight_grads)
        return (running, (result, stream_grad))
    starting = jax.tree.map(jnp.zeros_like, params)
    totals, (results, stream_grads) = lax.scan(one_sequence, starting, (streams, grads_in, seg_all, pos_all))
    return (results.reshape(TOKENS, D), stream_grads.reshape(TOKENS, D), totals[0], totals[1], totals[2], totals[3], totals[4], totals[5], totals[6], totals[7], totals[8])
```

```python
import jax
import jax.numpy as jnp
import numpy as np
from jax import lax
from jax.sharding import Mesh, PartitionSpec as P

HEAD_DIM = 128
LEN = 1024
BLOCK = 128
epsilon = 1e-05
base_freq = 10000.0
AXES = ("x", "ylo", "core", "yhi", "z")
SIZES = {"x": 4, "ylo": 2, "core": 2, "yhi": 2, "z": 4}
bf16 = jnp.bfloat16
f32 = jnp.float32
contract_last = (((1,), (1,)), ((), ()))
contract_first = (((0,), (0,)), ((), ()))


def swap_bits(value, axes, masks):
    sizes = [SIZES[a] for a in axes]
    pairs = []
    for index in np.ndindex(*sizes):
        target = tuple(i ^ m for i, m in zip(index, masks))
        pairs.append(
            (int(np.ravel_multi_index(index, sizes)), int(np.ravel_multi_index(target, sizes)))
        )
    return lax.ppermute(value, axes if len(axes) > 1 else axes[0], pairs)


def over_x(value, k):
    return swap_bits(value, ("x",), (k,))


def over_y(value, low, high):
    return swap_bits(value, ("ylo", "yhi"), (low, high))


def over_z(value, k):
    return swap_bits(value, ("z",), (k,))


def over_core(value):
    return swap_bits(value, ("core",), (1,))


def exchange(value):
    return lax.ppermute(value, ("core", "yhi"), [(0, 0), (1, 2), (2, 1), (3, 3)])


Y_STEPS = ((0, 1), (1, 0), (1, 1))


def gather_x_first(piece):
    row = jnp.concatenate([piece] + [over_x(piece, k) for k in (1, 2, 3)], axis=1)
    got = {(0, 0): row}
    for low, high in Y_STEPS:
        got[(low, high)] = over_y(row, low, high)
    return [
        jnp.concatenate(
            [got[(low, high)][:, 128 * i : 128 * i + 128] for i in range(4) for low in range(2)],
            axis=1,
        )
        for high in range(2)
    ]


def gather_y_first(piece):
    rows = piece.shape[0]
    got = {(0, 0): piece}
    for low, high in Y_STEPS:
        got[(low, high)] = over_y(piece, low, high)
    block = jnp.concatenate(
        [jnp.concatenate([got[(0, high)], got[(1, high)]], axis=1) for high in range(2)], axis=0
    )
    full = jnp.concatenate([block] + [over_x(block, k) for k in (1, 2, 3)], axis=1)
    return [full[:rows], full[rows:]]


def scatter_x_first(total):
    def part(low, high):
        return jnp.concatenate(
            [total[high][:, 256 * i + 128 * low : 256 * i + 128 * low + 128] for i in range(4)],
            axis=1,
        )

    acc = part(0, 0).astype(f32)
    for low, high in Y_STEPS:
        acc = acc + over_y(part(low, high).astype(bf16), low, high).astype(f32)
    out = acc[:, :128]
    for k in (1, 2, 3):
        out = out + over_x(acc[:, 128 * k : 128 * k + 128].astype(bf16), k).astype(f32)
    return out


def scatter_y_first(total):
    rows = total[0].shape[0]
    both = jnp.concatenate(total, axis=0)
    acc = both[:, :256].astype(f32)
    for k in (1, 2, 3):
        acc = acc + over_x(both[:, 256 * k : 256 * k + 256].astype(bf16), k).astype(f32)
    out = acc[:rows, :128]
    for low, high in Y_STEPS:
        out = out + over_y(
            acc[rows * high : rows * high + rows, 128 * low : 128 * low + 128].astype(bf16),
            low,
            high,
        ).astype(f32)
    return out


def gather_tokens(value):
    return jnp.concatenate([value] + [over_z(value, k) for k in (1, 2, 3)], axis=0)


def scatter_tokens(value):
    out = value[:BLOCK].astype(f32)
    for k in (1, 2, 3):
        out = out + over_z(value[BLOCK * k : BLOCK * k + BLOCK].astype(bf16), k).astype(f32)
    return out


def norm_forward(stream, gain):
    inverse = lax.rsqrt(jnp.mean(stream * stream, axis=-1, keepdims=True) + epsilon)
    return (stream * inverse * gain).astype(bf16), inverse


def norm_backward(stream, inverse, gain, gradient):
    scaled = gradient * gain
    mean_term = jnp.mean(scaled * stream, axis=-1, keepdims=True)
    back = inverse * scaled - stream * (inverse * inverse * inverse) * mean_term
    return back, jnp.sum(gradient * stream * inverse, axis=0)


def rotate(vectors, cosine, sine):
    first, second = jnp.split(vectors, 2, axis=-1)
    return jnp.concatenate([first * cosine - second * sine, second * cosine + first * sine], -1)


def dot_nt(left, halves):
    own, other = halves
    half = left.shape[1] // 2
    return lax.dot_general(
        left[:, :half], own, contract_last, preferred_element_type=f32
    ) + lax.dot_general(left[:, half:], other, contract_last, preferred_element_type=f32)


def dot_nn(left, halves):
    return jnp.concatenate(
        [jnp.dot(left, w, preferred_element_type=f32).astype(bf16) for w in halves], axis=1
    )


def grad_halves(left, right):
    half = right.shape[1] // 2
    away = lax.dot_general(
        left, right[:, half:], contract_first, preferred_element_type=f32
    ).astype(bf16)
    here = lax.dot_general(left, right[:, :half], contract_first, preferred_element_type=f32)
    return here + over_core(away).astype(f32)


def body(
    block_input,
    segments,
    positions,
    attn_gain,
    w_query,
    w_key,
    w_value,
    w_output,
    mlp_gain,
    w_gate,
    w_up,
    w_down,
    cotangent,
):
    at_x, at_ylo, at_core, at_yhi, at_z = (lax.axis_index(a) for a in AXES)
    width = w_query.shape[1]
    hidden_local = w_gate.shape[1]
    first_core = at_core == 0

    def reorder(value):
        parts = []
        for k in range(2):
            for i in range(4):
                for j in range(2):
                    index = (at_x ^ i) * 4 + (at_ylo ^ j) * 2 + (at_core ^ k)
                    parts.append(lax.dynamic_slice_in_dim(value, index * 128, 128, axis=-1))
        return jnp.concatenate(parts, axis=-1)

    def restore(value):
        parts = []
        for x in range(4):
            for y in range(2):
                for c in range(2):
                    index = (at_core ^ c) * 8 + (at_x ^ x) * 2 + (at_ylo ^ y)
                    parts.append(lax.dynamic_slice_in_dim(value, index * 128, 128, axis=-1))
        return jnp.concatenate(parts, axis=-1)

    piece_qk = jnp.concatenate([w_query.T, w_key.T], axis=0)
    piece_vo = jnp.concatenate([w_value.T, w_output], axis=0)
    cut = 352
    piece_gd = jnp.concatenate([w_gate.T, w_down[:cut]], axis=0)
    piece_ud = jnp.concatenate([w_up.T, w_down[cut:]], axis=0)

    stream = reorder(exchange(block_input))
    grad_low = reorder(exchange(cotangent.astype(bf16)))
    tables = jnp.stack([segments, positions])
    tables = jnp.where(at_core == at_yhi, tables, over_core(tables))
    gain1 = reorder(attn_gain)
    gain2 = reorder(mlp_gain)

    qk = gather_x_first(piece_qk)
    vo = gather_y_first(piece_vo)

    def both(parts):
        own = jnp.concatenate(parts, axis=0)
        return own, over_core(own)

    weight_q = both([p[:width] for p in qk])
    weight_k = both([p[width:] for p in qk])
    weight_v = both([p[:width] for p in vo])
    weight_o = both([p[width:] for p in vo])

    act1, inverse1 = norm_forward(stream, gain1)
    act1_all = gather_tokens(act1)

    order = [(at_core ^ h) * 4 + (at_z ^ k) for h in range(2) for k in range(4)]
    tables = jnp.concatenate(
        [lax.dynamic_slice_in_dim(tables, o * BLOCK, BLOCK, axis=1) for o in order], axis=1
    )
    place = jnp.concatenate([o * BLOCK + jnp.arange(BLOCK, dtype=jnp.int32) for o in order])
    seg_rows, pos_rows = tables[0], tables[1]
    frequency = base_freq ** (-(2.0 * jnp.arange(HEAD_DIM // 2, dtype=f32)) / HEAD_DIM)
    angles = pos_rows[:512].astype(f32)[:, None] * frequency[None, :]
    cosine, sine = jnp.cos(angles)[:, None, :], jnp.sin(angles)[:, None, :]

    def heads(value):
        return value.reshape(512, -1, HEAD_DIM)

    q = rotate(heads(dot_nt(act1_all, weight_q)), cosine, sine).astype(bf16)
    k = rotate(heads(dot_nt(act1_all, weight_k)), cosine, sine).astype(bf16)
    v = heads(dot_nt(act1_all, weight_v)).astype(bf16)
    qkv = jnp.stack([q, k, v]).reshape(3, 512, 2, 2, HEAD_DIM)
    keep = jnp.where(first_core, qkv[:, :, 0], qkv[:, :, 1])
    away = jnp.where(first_core, qkv[:, :, 1], qkv[:, :, 0])
    qkv = jnp.concatenate([keep, over_core(away)], axis=1)
    queries, keys, values = qkv[0], qkv[1], qkv[2]

    allowed = (seg_rows[:, None] == seg_rows[None, :]) & (place[None, :] <= place[:, None])
    scale = HEAD_DIM**-0.5
    logits = jnp.einsum("qhd,khd->hqk", queries, keys, preferred_element_type=f32) * scale
    logits = jnp.where(allowed[None], logits, -1e30)
    row_max = jnp.max(logits, axis=-1, keepdims=True)
    exponent = jnp.exp(logits - row_max)
    probs = exponent / jnp.sum(exponent, axis=-1, keepdims=True)
    probs_low = probs.astype(bf16)
    attended = jnp.einsum("hqk,khd->qhd", probs_low, values, preferred_element_type=f32)
    attended = attended.astype(bf16).reshape(1024, 2 * HEAD_DIM)

    def rejoin(value):
        mine = value[..., :512, :]
        got = over_core(value[..., 512:, :])
        return jnp.concatenate(
            [jnp.where(first_core, mine, got), jnp.where(first_core, got, mine)], axis=-1
        )

    attended_rows = rejoin(attended)
    middle = stream + scatter_tokens(dot_nn(attended_rows, weight_o))
    act2, inverse2 = norm_forward(middle, gain2)
    act2_all = gather_tokens(act2)

    gd = gather_x_first(piece_gd)
    ud = gather_y_first(piece_ud)
    weight_g = both([p[:hidden_local] for p in gd])
    weight_u = both([p[:hidden_local] for p in ud])
    weight_d = both([p[hidden_local:] for pair in zip(gd, ud) for p in pair])

    grad_all = gather_tokens(grad_low)
    hidden_grad = dot_nt(grad_all, weight_d)
    gate = dot_nt(act2_all, weight_g)
    up = dot_nt(act2_all, weight_u)
    sigmoid = jax.nn.sigmoid(gate)
    silu = gate * sigmoid
    hidden = (silu * up).astype(bf16)
    gate_grad = (hidden_grad * up * sigmoid * (1.0 + gate * (1.0 - sigmoid))).astype(bf16)
    up_grad = (hidden_grad * silu).astype(bf16)

    out_block = middle + scatter_tokens(dot_nn(hidden, weight_d))
    grad_act2 = scatter_tokens(
        jnp.concatenate(
            [
                (
                    jnp.dot(gate_grad, wg, preferred_element_type=f32)
                    + jnp.dot(up_grad, wu, preferred_element_type=f32)
                ).astype(bf16)
                for wg, wu in zip(weight_g, weight_u)
            ],
            axis=1,
        )
    )
    sum_g = grad_halves(gate_grad, act2_all)
    sum_u = grad_halves(up_grad, act2_all)
    sum_d = grad_halves(hidden, grad_all)
    n = hidden_local
    grad_gd = scatter_x_first(
        [jnp.concatenate([sum_g[h * n : h * n + n], sum_d[h * n : h * n + cut]]) for h in range(2)]
    )
    grad_ud = scatter_y_first(
        [
            jnp.concatenate([sum_u[h * n : h * n + n], sum_d[h * n + cut : h * n + n]])
            for h in range(2)
        ]
    )
    grad_gate = grad_gd[:n].T
    grad_up = grad_ud[:n].T
    grad_down = jnp.concatenate([grad_gd[n:], grad_ud[n:]], axis=0)

    middle_back, gain2_part = norm_backward(middle, inverse2, gain2, grad_act2)
    grad_middle = grad_low.astype(f32) + middle_back
    middle_low = grad_middle.astype(bf16)
    middle_all = gather_tokens(middle_low)
    attended_grad = dot_nt(middle_all, weight_o).astype(bf16)
    sum_o = grad_halves(attended_rows, middle_all)
    split = attended_grad.reshape(512, 2, 256)
    keep = jnp.where(first_core, split[:, 0], split[:, 1])
    away = jnp.where(first_core, split[:, 1], split[:, 0])
    attended_grad = jnp.concatenate([keep, over_core(away)], axis=0).reshape(1024, 2, HEAD_DIM)

    grad_probs = jnp.einsum("qhd,khd->hqk", attended_grad, values, preferred_element_type=f32)
    inner = jnp.sum(probs * grad_probs, axis=-1, keepdims=True)
    score_grad = (probs * (grad_probs - inner)).astype(bf16)
    query_grad = jnp.einsum("hqk,khd->qhd", score_grad, keys, preferred_element_type=f32) * scale
    key_grad = jnp.einsum("hqk,qhd->khd", score_grad, queries, preferred_element_type=f32) * scale
    value_grad = jnp.einsum("hqk,qhd->khd", probs_low, attended_grad, preferred_element_type=f32)
    angles = pos_rows.astype(f32)[:, None] * frequency[None, :]
    cosine, sine = jnp.cos(angles)[:, None, :], jnp.sin(angles)[:, None, :]
    grads = jnp.stack(
        [
            rotate(query_grad, cosine, -sine).astype(bf16),
            rotate(key_grad, cosine, -sine).astype(bf16),
            value_grad.astype(bf16),
        ]
    ).reshape(3, 1024, 2 * HEAD_DIM)
    q_low, k_low, v_low = rejoin(grads)
    grad_act1 = scatter_tokens(
        jnp.concatenate(
            [
                sum(
                    jnp.dot(g, w, preferred_element_type=f32)
                    for g, w in ((q_low, wq), (k_low, wk), (v_low, wv))
                ).astype(bf16)
                for wq, wk, wv in zip(weight_q, weight_k, weight_v)
            ],
            axis=1,
        )
    )
    sum_q = grad_halves(q_low, act1_all)
    sum_k = grad_halves(k_low, act1_all)
    sum_v = grad_halves(v_low, act1_all)
    w = width
    grad_qk = scatter_x_first(
        [jnp.concatenate([sum_q[h * w : h * w + w], sum_k[h * w : h * w + w]]) for h in range(2)]
    )
    grad_vo = scatter_y_first(
        [jnp.concatenate([sum_v[h * w : h * w + w], sum_o[h * w : h * w + w]]) for h in range(2)]
    )
    input_back, gain1_part = norm_backward(stream, inverse1, gain1, grad_act1)
    grad_input = exchange(restore(grad_middle + input_back).astype(bf16)).astype(f32)
    out_block = exchange(restore(out_block))

    gains = restore(jnp.stack([gain1_part, gain2_part]))

    def add_four(value, step):
        one, two, three = (step(value, i) for i in range(3))
        return (value + one) + (two + three)

    gains = add_four(gains, lambda v, i: over_z(v, i + 1))
    gains = add_four(gains, lambda v, i: over_y(v, *((0, 1), (1, 0), (1, 1))[i]))
    gains = add_four(gains, lambda v, i: over_x(v, i + 1))
    gains = gains + over_core(gains)
    return (
        out_block,
        grad_input,
        gains[0],
        grad_qk[:w].T,
        grad_qk[w:].T,
        grad_vo[:w].T,
        grad_vo[w:],
        gains[1],
        grad_gate,
        grad_up,
        grad_down,
    )


def solution(mesh):
    inner = Mesh(np.asarray(mesh.devices).reshape([SIZES[a] for a in AXES]), AXES)
    dp, tensor = ("x", "ylo", "core"), ("yhi", "z")
    rows = P(dp + tensor, None)
    return jax.shard_map(
        body,
        mesh=inner,
        in_specs=(
            rows,
            P(dp),
            P(dp),
            P(),
            P(dp, tensor),
            P(dp, tensor),
            P(dp, tensor),
            P(tensor, dp),
            P(),
            P(dp, tensor),
            P(dp, tensor),
            P(tensor, dp),
            rows,
        ),
        out_specs=(
            rows,
            rows,
            P(),
            P(dp, tensor),
            P(dp, tensor),
            P(dp, tensor),
            P(tensor, dp),
            P(),
            P(dp, tensor),
            P(dp, tensor),
            P(tensor, dp),
        ),
        check_vma=False,
    )
```

```python
import functools

import jax
import jax.numpy as jnp
import numpy as np
from jax import lax
from jax.experimental import pallas as pl
from jax.experimental.pallas import tpu as pltpu
from jax.sharding import Mesh, PartitionSpec as P

HEAD_DIM = 128
BLOCK = 128
D = 2048
UNITS = 688
WIDTH = 256
epsilon = 1e-05
base_freq = 10000.0
AXES = ("x", "ylo", "core", "yhi", "z")
SIZES = {"x": 4, "ylo": 2, "core": 2, "yhi": 2, "z": 4}
bf16 = jnp.bfloat16
f32 = jnp.float32
MIB = 1 << 20
VMEM = pl.BlockSpec(memory_space=pltpu.VMEM)
SMEM = pl.BlockSpec(memory_space=pltpu.SMEM)
ANY = pl.BlockSpec(memory_space=pl.ANY)


def dot_nn(a, b):
    return lax.dot_general(a, b, (((1,), (0,)), ((), ())), preferred_element_type=f32)


def dot_nt(a, b):
    return lax.dot_general(a, b, (((1,), (1,)), ((), ())), preferred_element_type=f32)


def dot_tn(a, b):
    return lax.dot_general(a, b, (((0,), (0,)), ((), ())), preferred_element_type=f32)


def call(kernel, ins, outs, scratch, operands, flops=0, limit=56, after=()):
    nbytes = sum(o.size * o.dtype.itemsize for o in operands)
    count, skip = len(operands), len(after)

    def run(*refs):
        kernel(*refs[:count], *refs[count + skip :])

    operands = [*operands, *after]
    ins = [*ins] + [ANY] * skip
    return pl.pallas_call(
        run,
        in_specs=ins,
        out_specs=[o[1] for o in outs],
        out_shape=[o[0] for o in outs],
        scratch_shapes=scratch,
        compiler_params=pltpu.CompilerParams(vmem_limit_bytes=limit * MIB),
        cost_estimate=pl.CostEstimate(
            flops=flops // 6, bytes_accessed=nbytes // 6, transcendentals=0
        ),
    )(*operands)


def shape(*dims, dtype=bf16):
    return jax.ShapeDtypeStruct(dims, dtype)


def load_pieces(place, pieces, target, first, rows, sem):
    for j in range(8):
        for i in range(4):
            at = place[2 * (4 * j + i)]
            lane = pl.multiple_of(place[2 * (4 * j + i) + 1] * 128, 128)
            pltpu.make_async_copy(
                pieces[j].at[i, pl.ds(first, rows), :],
                target.at[at, :, pl.ds(lane, 128)],
                sem,
            ).start()


def fill(info, blocks, target):
    for k in range(4):
        at = pl.multiple_of((info[1] ^ k) * BLOCK, BLOCK)
        target[pl.ds(at, BLOCK), :] = blocks[k][...]


def wait_all(target, sem):
    pltpu.make_async_copy(target, target, sem).wait()


def qkv_kernel(info, *refs):
    act, pieces = refs[0], refs[1:9]
    cosine, sine, keep, away, weight, sem = *refs[9:12], refs[12:15], *refs[15:]
    core = info[0]
    load_pieces(info.at[pl.ds(8, 64)], pieces, weight, 0, 768, sem)
    wait_all(weight, sem)
    for which, out in ((1, away), (0, keep)):
        s = core ^ which
        for m in range(3):
            got = dot_nt(act[...], weight[s, pl.ds(WIDTH * m, WIDTH), :])
            place = out.at[m] if which == 0 else out[m]
            if m == 2:
                place[...] = got.astype(bf16)
                continue
            for h in range(2):
                v = got[:, HEAD_DIM * h : HEAD_DIM * h + HEAD_DIM]
                turned = pltpu.roll(v, HEAD_DIM // 2, 1)
                place[:, HEAD_DIM * h : HEAD_DIM * h + HEAD_DIM] = (
                    v * cosine[...] + turned * sine[...]
                ).astype(bf16)


def project_qkv(info, act, pieces, cosine, sine, after=()):
    return call(
        qkv_kernel,
        [SMEM] + [VMEM] + [ANY] * 8 + [VMEM] * 2,
        [(shape(3, 512, WIDTH), VMEM)] + [(shape(512, WIDTH), VMEM)] * 3,
        [pltpu.VMEM((2, 768, D), bf16), pltpu.SemaphoreType.DMA],
        [info, act, *pieces, cosine, sine],
        flops=2 * 512 * D * 1536,
        after=after,
    )


TILE = 256


def masked_scores(q, k, seg_col, seg_row, first, count):
    s = dot_nt(q, k) * HEAD_DIM**-0.5
    rows = first + lax.broadcasted_iota(jnp.int32, (TILE, count), 0)
    cols = lax.broadcasted_iota(jnp.int32, (TILE, count), 1)
    ok = (cols <= rows) & (seg_col == seg_row)
    return jnp.where(ok, s, -1e30)


def softmax(s):
    e = jnp.exp(s - jnp.max(s, axis=-1, keepdims=True))
    return e * (1.0 / jnp.sum(e, axis=-1, keepdims=True))


def to_order(info, mine, got, target, m):
    for h, source in ((0, mine.at[m]), (1, got)):
        at = pl.multiple_of((info[0] ^ h) * 512, 512)
        target[m, pl.ds(at, 512), :] = source[...]


def from_order(info, source, m, target, h):
    at = pl.multiple_of((info[0] ^ h) * 512, 512)
    target[m] = source[m, pl.ds(at, 512), :]


def attend_kernel(info, mine, *refs):
    got, (seg_col, seg_row, keep, away, qkv, result) = refs[:3], refs[3:]
    for m in range(3):
        to_order(info, mine, got[m], qkv, m)
    for h in range(2):
        lanes = slice(HEAD_DIM * h, HEAD_DIM * h + HEAD_DIM)
        for t in range(1024 // TILE):
            n = TILE * (t + 1)
            rows = slice(TILE * t, n)
            s = masked_scores(
                qkv[0, rows, lanes], qkv[1, :n, lanes], seg_col[rows, :], seg_row[:, :n],
                TILE * t, n,
            )
            result[0, rows, lanes] = dot_nn(softmax(s).astype(bf16), qkv[2, :n, lanes]).astype(bf16)
    from_order(info, result, 0, away, 1)
    from_order(info, result, 0, keep, 0)


def attend(info, mine, got, seg_col, seg_row, after=()):
    return call(
        attend_kernel,
        [SMEM] + [VMEM] * 6,
        [(shape(1, 512, WIDTH), VMEM)] * 2,
        [pltpu.VMEM((3, 1024, WIDTH), bf16), pltpu.VMEM((1, 1024, WIDTH), bf16)],
        [info, mine, *got, seg_col, seg_row],
        flops=4 * 2 * 1024 * 1024 * 128,
        after=after,
    )


def attend_back_kernel(info, mine, *refs):
    got, (g_mine, g_got, seg_col, seg_row, cosine, sine, keep, away) = refs[:3], refs[3:11]
    qkv, grad, total, result = refs[11:]
    scale = HEAD_DIM**-0.5
    for m in range(3):
        to_order(info, mine, got[m], qkv, m)
    to_order(info, g_mine, g_got.at[0], grad, 0)
    for h in range(2):
        lanes = slice(HEAD_DIM * h, HEAD_DIM * h + HEAD_DIM)
        total[...] = jnp.zeros_like(total)
        for t in range(1024 // TILE):
            n = TILE * (t + 1)
            rows = slice(TILE * t, n)
            q, g = qkv[0, rows, lanes], grad[0, rows, lanes]
            s = masked_scores(q, qkv[1, :n, lanes], seg_col[rows, :], seg_row[:, :n], TILE * t, n)
            p = softmax(s)
            dp = dot_nt(g, qkv[2, :n, lanes])
            ds = (p * (dp - jnp.sum(p * dp, axis=-1, keepdims=True))).astype(bf16)
            total[0, rows, :] = dot_nn(ds, qkv[1, :n, lanes]) * scale
            total[1, :n, :] += dot_tn(ds, q) * scale
            total[2, :n, :] += dot_tn(p.astype(bf16), g)
        for m in range(2):
            v = total[m]
            turned = pltpu.roll(v, HEAD_DIM // 2, 1)
            result[m, :, lanes] = (v * cosine[...] - turned * sine[...]).astype(bf16)
        result[2, :, lanes] = total[2].astype(bf16)
    for m in range(3):
        from_order(info, result, m, away, 1)
        from_order(info, result, m, keep, 0)


def attend_back(info, mine, got, g_mine, g_got, seg_col, seg_row, cosine, sine, after=()):
    return call(
        attend_back_kernel,
        [SMEM] + [VMEM] * 10,
        [(shape(3, 512, WIDTH), VMEM)] * 2,
        [
            pltpu.VMEM((3, 1024, WIDTH), bf16),
            pltpu.VMEM((1, 1024, WIDTH), bf16),
            pltpu.VMEM((3, 1024, HEAD_DIM), f32),
            pltpu.VMEM((3, 1024, WIDTH), bf16),
        ],
        [info, mine, *got, g_mine, g_got, seg_col, seg_row, cosine, sine],
        flops=10 * 2 * 1024 * 1024 * 128,
        after=after,
    )


def write_blocks(info, total, outs):
    for k in range(4):
        at = pl.multiple_of((info[1] ^ k) * BLOCK, BLOCK)
        outs[k][...] = total[pl.ds(at, BLOCK), :].astype(outs[k].dtype)


TOTAL = pltpu.VMEM((512, D), f32)
BLOCK_OUTS = [(shape(BLOCK, D, dtype=f32), VMEM)] + [(shape(BLOCK, D), VMEM)] * 3


def out_kernel(info, mine, got, *refs):
    pieces, outs, (weight, total, sem) = refs[:8], refs[8:12], refs[12:]
    core = info[0]
    load_pieces(info.at[pl.ds(8, 64)], pieces, weight, 768, 256, sem)
    wait_all(weight, sem)
    total[...] = dot_nn(mine[0], weight[core]) + dot_nn(got[0], weight[core ^ 1])
    write_blocks(info, total, outs)


def project_out(info, mine, got, pieces, after=()):
    return call(
        out_kernel,
        [SMEM] + [VMEM] * 2 + [ANY] * 8,
        BLOCK_OUTS,
        [pltpu.VMEM((2, 256, D), bf16), TOTAL, pltpu.SemaphoreType.DMA],
        [info, mine, got, *pieces],
        flops=2 * 512 * D * 512,
        after=after,
    )


def out_back_kernel(info, *refs):
    act, pieces = refs[0], refs[1:9]
    keep, away, weight, sem = refs[9:]
    core = info[0]
    load_pieces(info.at[pl.ds(8, 64)], pieces, weight, 768, 256, sem)
    wait_all(weight, sem)
    for which, out in ((1, away), (0, keep)):
        out[0] = dot_nt(act[...], weight[core ^ which]).astype(bf16)


def project_out_back(info, act, pieces, after=()):
    return call(
        out_back_kernel,
        [SMEM] + [VMEM] + [ANY] * 8,
        [(shape(1, 512, WIDTH), VMEM)] * 2,
        [pltpu.VMEM((2, 256, D), bf16), pltpu.SemaphoreType.DMA],
        [info, act, *pieces],
        flops=2 * 512 * D * 512,
        after=after,
    )


def qkv_back_kernel(info, mine, got, *refs):
    pieces, act, out, gain, weight, total, sem = refs[:8], *refs[8:]
    core = info[0]
    load_pieces(info.at[pl.ds(8, 64)], pieces, weight, 0, 768, sem)
    wait_all(weight, sem)
    for which, source in ((0, mine), (1, got)):
        for m in range(3):
            part = dot_nn(source[m], weight[core ^ which, pl.ds(WIDTH * m, WIDTH), :])
            if which == 0 and m == 0:
                total[...] = part
            else:
                total[...] += part
    out[...] = total[...].astype(bf16)
    gain[...] = jnp.sum(total[...] * act[...].astype(f32), axis=0, keepdims=True)


def project_qkv_back(info, mine, got, pieces, act, after=()):
    return call(
        qkv_back_kernel,
        [SMEM] + [VMEM] * 2 + [ANY] * 8 + [VMEM],
        [(shape(512, D), VMEM), (shape(1, D, dtype=f32), VMEM)],
        [pltpu.VMEM((2, 768, D), bf16), TOTAL, pltpu.SemaphoreType.DMA],
        [info, mine, got, *pieces, act],
        flops=2 * 512 * D * 1536,
        after=after,
    )


def load_gathered(weights, target, first, rows, sems):
    for s in range(2):
        for x in range(4):
            for y in range(2):
                for c in range(2):
                    f = x * 4 + y * 2 + c
                    pltpu.make_async_copy(
                        weights.at[x * 8 + y * 4 + s * 2 + c, pl.ds(first, rows), :],
                        target.at[s, :, f * 128 : f * 128 + 128],
                        sems.at[s],
                    ).start()


def mlp_kernel(info, *refs):
    acts, cots, weights = refs[:4], refs[4:8], refs[8]
    hid, gate_grad, up_grad, out = refs[9:13]
    weight, act, cot, total, sems = refs[13:]
    load_gathered(weights, weight, 0, 3 * UNITS, sems)
    fill(info, acts, act)
    fill(info, cots, cot)
    for s in range(2):
        wait_all(weight.at[s], sems.at[s])
        gate = dot_nt(act[...], weight[s, pl.ds(0, UNITS), :])
        up = dot_nt(act[...], weight[s, pl.ds(UNITS, UNITS), :])
        hg = dot_nt(cot[...], weight[s, pl.ds(2 * UNITS, UNITS), :])
        sig = 1.0 / (1.0 + jnp.exp(-gate))
        silu = gate * sig
        hid[s] = (silu * up).astype(bf16)
        gate_grad[s] = (hg * up * (sig * (1.0 + gate * (1.0 - sig)))).astype(bf16)
        up_grad[s] = (hg * silu).astype(bf16)
        part = dot_nn(gate_grad[s], weight[s, pl.ds(0, UNITS), :]) + dot_nn(
            up_grad[s], weight[s, pl.ds(UNITS, UNITS), :]
        )
        if s == 0:
            total[...] = part
        else:
            out[...] = (total[...] + part).astype(bf16)


def mlp(info, acts, cots, weights, after=()):
    return call(
        mlp_kernel,
        [SMEM] + [VMEM] * 8 + [ANY],
        [(shape(2, 512, UNITS), VMEM)] * 3 + [(shape(512, D), VMEM)],
        [
            pltpu.VMEM((2, 3 * UNITS, D), bf16),
            pltpu.VMEM((512, D), bf16),
            pltpu.VMEM((512, D), bf16),
            pltpu.VMEM((512, D), f32),
            pltpu.SemaphoreType.DMA((2,)),
        ],
        [info, *acts, *cots, weights],
        flops=2 * 512 * D * 1376 * 5,
        after=after,
    )


def down_kernel(hid, weights, out, weight, total, sems):
    load_gathered(weights, weight, 2 * UNITS, UNITS, sems)
    wait_all(weight.at[0], sems.at[0])
    total[...] = dot_nn(hid[0], weight[0])
    wait_all(weight.at[1], sems.at[1])
    total[...] += dot_nn(hid[1], weight[1])
    for k in range(4):
        out[k] = total[BLOCK * k : BLOCK * k + BLOCK, :].astype(bf16)


def project_down(hid, weights, after=()):
    return call(
        down_kernel,
        [VMEM, ANY],
        [(shape(4, BLOCK, D), VMEM)],
        [
            pltpu.VMEM((2, UNITS, D), bf16),
            pltpu.VMEM((512, D), f32),
            pltpu.SemaphoreType.DMA((2,)),
        ],
        [hid, weights],
        flops=2 * 512 * D * 1376,
        after=after,
    )


def half_features(info, source, target, which):
    core, x, y = info[0], info[2], info[3]
    for dx in range(4):
        for dlo in range(2):
            lane = ((x ^ dx) * 4 + (y ^ dlo) * 2 + (core ^ which)) * 128
            b = 2 * dx + dlo
            target[:, 128 * b : 128 * b + 128] = source[:, pl.ds(pl.multiple_of(lane, 128), 128)]


def away_grads(info, lefts, rights, units, away, stage, sems):
    to_core = info[0] ^ 1
    step = 0
    for h in range(2):
        for m, right in enumerate(rights):
            slot = step % 2
            if step >= 2:
                wait_all(stage.at[slot], sems.at[slot])
            part = dot_tn(lefts(h, m), right[...]).astype(bf16)
            for dx in range(4):
                for dlo in range(2):
                    b, dy = 2 * dx + dlo, dlo + 2 * h
                    stage[slot, b] = part[:, 128 * b : 128 * b + 128]
                    i = jnp.where(to_core == 0, dx, dy)
                    j = jnp.where(to_core == 0, dy, dx)
                    pltpu.make_async_copy(
                        stage.at[slot, b], away.at[j, i, pl.ds(units * m, units), :], sems.at[slot]
                    ).start()
            step += 1
    for slot in range(2):
        wait_all(stage.at[slot], sems.at[slot])


def here_grads(info, lefts, rights, units, got_hbm, outs, got, stage, sems, got_sem):
    core = info[0]
    load = pltpu.make_async_copy(got_hbm, got, got_sem)
    load.start()
    step = 0
    for h in range(2):
        for m, right in enumerate(rights):
            slot = step % 2
            part = dot_tn(lefts(h, m), right[...])
            if step == 0:
                load.wait()
            if step >= 2:
                wait_all(stage.at[slot], sems.at[slot])
            rows = pl.ds(units * m, units)
            for dx in range(4):
                for dlo in range(2):
                    b, dy = 2 * dx + dlo, dlo + 2 * h
                    i = jnp.where(core == 0, dx, dy)
                    j = jnp.where(core == 0, dy, dx)
                    stage[slot, b] = (
                        part[:, 128 * b : 128 * b + 128] + got[j, i, rows, :].astype(f32)
                    ).astype(bf16)

            def send(on_core):
                for dx in range(4):
                    for dlo in range(2):
                        b, dy = 2 * dx + dlo, dlo + 2 * h
                        i, j = (dx, dy) if on_core == 0 else (dy, dx)
                        pltpu.make_async_copy(
                            stage.at[slot, b], outs[j].at[i, rows, :], sems.at[slot]
                        ).start()

            pl.when(core == 0)(functools.partial(send, 0))
            pl.when(core == 1)(functools.partial(send, 1))
            step += 1
    for slot in range(2):
        wait_all(stage.at[slot], sems.at[slot])


def mlp_rights(info, act, cot, act_half, cot_half, which):
    half_features(info, act, act_half, which)
    half_features(info, cot, cot_half, which)
    return act_half, act_half, cot_half


def mlp_away_kernel(info, hid, gate_grad, up_grad, *refs):
    acts, cots = refs[:4], refs[4:8]
    away, act, cot, act_half, cot_half, stage, sems = refs[8:]
    fill(info, acts, act)
    fill(info, cots, cot)
    rights = mlp_rights(info, act, cot, act_half, cot_half, 1)
    sources = (gate_grad, up_grad, hid)
    away_grads(
        info, lambda h, m: sources[m][info[4] ^ h], rights, UNITS, away, stage, sems
    )


def mlp_here_kernel(info, hid, gate_grad, up_grad, *refs):
    acts, cots, got_hbm, outs = refs[:4], refs[4:8], refs[8], refs[9:13]
    act, cot, act_half, cot_half, got, stage, sems, got_sem = refs[13:]
    fill(info, acts, act)
    fill(info, cots, cot)
    rights = mlp_rights(info, act, cot, act_half, cot_half, 0)
    sources = (gate_grad, up_grad, hid)
    here_grads(
        info, lambda h, m: sources[m][info[4] ^ h], rights, UNITS, got_hbm, outs,
        got, stage, sems, got_sem,
    )


ROWS = pltpu.VMEM((512, D), bf16)
HALF = pltpu.VMEM((512, D // 2), bf16)


def mlp_away(info, hid, gate_grad, up_grad, acts, cots, after=()):
    return call(
        mlp_away_kernel,
        [SMEM] + [VMEM] * 11,
        [(shape(4, 4, 3 * UNITS, 128), ANY)],
        [ROWS, ROWS, HALF, HALF, pltpu.VMEM((2, 8, UNITS, 128), bf16),
         pltpu.SemaphoreType.DMA((2,))],
        [info, hid, gate_grad, up_grad, *acts, *cots],
        flops=512 * D * 1376 * 3,
        after=after,
    )[0]


def mlp_here(info, hid, gate_grad, up_grad, acts, cots, got, after=()):
    return call(
        mlp_here_kernel,
        [SMEM] + [VMEM] * 11 + [ANY],
        [(shape(4, 3 * UNITS, 128), ANY)] * 4,
        [ROWS, ROWS, HALF, HALF, pltpu.VMEM((4, 4, 3 * UNITS, 128), bf16),
         pltpu.VMEM((2, 8, UNITS, 128), bf16),
         pltpu.SemaphoreType.DMA((2,)), pltpu.SemaphoreType.DMA],
        [info, hid, gate_grad, up_grad, *acts, *cots, got],
        flops=512 * D * 1376 * 3,
        after=after,
    )


def join_lefts(mine, got, att_mine, att_got, left):
    for w, (grads, att) in enumerate(((mine, att_mine), (got, att_got))):
        left[w, 0:3] = grads[...]
        left[w, 3] = att[0]


def attn_away_kernel(info, mine, got, att_mine, att_got, act, mid, *refs):
    away, left, act_half, mid_half, stage, sems = refs
    join_lefts(mine, got, att_mine, att_got, left)
    half_features(info, act, act_half, 1)
    half_features(info, mid, mid_half, 1)
    away_grads(
        info, lambda h, m: left[info[0] ^ info[4] ^ h, m],
        (act_half, act_half, act_half, mid_half), WIDTH, away, stage, sems,
    )


def attn_here_kernel(info, mine, got, att_mine, att_got, act, mid, got_hbm, *refs):
    outs, (left, act_half, mid_half, got_sum, stage, sems, got_sem) = refs[:4], refs[4:]
    join_lefts(mine, got, att_mine, att_got, left)
    half_features(info, act, act_half, 0)
    half_features(info, mid, mid_half, 0)
    here_grads(
        info, lambda h, m: left[info[0] ^ info[4] ^ h, m],
        (act_half, act_half, act_half, mid_half), WIDTH, got_hbm, outs,
        got_sum, stage, sems, got_sem,
    )


LEFT = pltpu.VMEM((2, 4, 512, WIDTH), bf16)


def attn_away(info, operands, after=()):
    return call(
        attn_away_kernel,
        [SMEM] + [VMEM] * 6,
        [(shape(4, 4, 4 * WIDTH, 128), ANY)],
        [LEFT, HALF, HALF, pltpu.VMEM((2, 8, WIDTH, 128), bf16), pltpu.SemaphoreType.DMA((2,))],
        [info, *operands],
        flops=512 * D * 2048,
        after=after,
    )[0]


def attn_here(info, operands, got, after=()):
    return call(
        attn_here_kernel,
        [SMEM] + [VMEM] * 6 + [ANY],
        [(shape(4, 4 * WIDTH, 128), ANY)] * 4,
        [LEFT, HALF, HALF, pltpu.VMEM((4, 4, 4 * WIDTH, 128), bf16),
         pltpu.VMEM((2, 8, WIDTH, 128), bf16),
         pltpu.SemaphoreType.DMA((2,)), pltpu.SemaphoreType.DMA],
        [info, *operands, got],
        flops=512 * D * 2048,
        after=after,
    )


def norm_back(x, gain, gradient):
    inverse = lax.rsqrt(jnp.mean(x * x, axis=-1, keepdims=True) + epsilon)
    scaled = gradient * gain
    mean_term = jnp.mean(scaled * x, axis=-1, keepdims=True)
    back = inverse * scaled - x * (inverse * inverse * inverse) * mean_term
    return back, inverse


def middle_back_kernel(middle, gain, gradient, cotangent, out, low, gain_part):
    x, e = middle[...], gradient[...].astype(f32)
    back, inverse = norm_back(x, gain[...], e)
    total = cotangent[...].astype(f32) + back
    out[...] = total
    low[...] = total.astype(bf16)
    gain_part[...] = jnp.sum(e * x * inverse, axis=0, keepdims=True)


def middle_back(middle, gain, gradient, cotangent, after):
    return call(
        middle_back_kernel,
        [VMEM] * 4,
        [
            (shape(BLOCK, D, dtype=f32), VMEM),
            (shape(BLOCK, D), VMEM),
            (shape(1, D, dtype=f32), VMEM),
        ],
        [],
        [middle, gain[None], gradient, cotangent],
        after=after,
    )


def input_back_kernel(stream, gain, gradient, middle, out):
    back, _ = norm_back(stream[...].astype(f32), gain[...], gradient[...].astype(f32))
    out[...] = (middle[...] + back).astype(bf16)


def input_back(stream, gain, gradient, middle):
    return call(
        input_back_kernel,
        [VMEM] * 4,
        [(shape(BLOCK, D), VMEM)],
        [],
        [stream, gain[None], gradient, middle],
    )[0]


def second_sum_kernel(*refs):
    ins, outs = refs[:4], refs[4:]
    for k in range(4):
        total = ins[0][k].astype(f32)
        for v in ins[1:]:
            total = total + v[k].astype(f32)
        outs[k][...] = total.astype(outs[k].dtype)


def second_sum(parts, after=()):
    rows = parts[0].shape[1]
    cut = rows // 3 if rows % 3 == 0 else rows // 2
    count = len(after)

    def run(*refs):
        second_sum_kernel(*refs[:4], *refs[4 + count :])

    whole = pl.BlockSpec((4, cut, 128), lambda r: (0, r, 0))
    part = pl.BlockSpec((cut, 128), lambda r: (r, 0))
    return pl.pallas_call(
        run,
        grid=(rows // cut,),
        in_specs=[whole] * 4 + [ANY] * count,
        out_specs=[part] * 4,
        out_shape=[shape(rows, 128, dtype=f32)] + [shape(rows, 128)] * 3,
        cost_estimate=pl.CostEstimate(flops=0, bytes_accessed=rows * 1024, transcendentals=0),
        compiler_params=pltpu.CompilerParams(vmem_limit_bytes=32 * MIB),
    )(*parts, *after)


def stack_kernel(*refs):
    gate, up, down, out = refs[0], refs[1], refs[2], refs[-1]
    out[0:UNITS, :] = gate[...].T
    out[UNITS : 2 * UNITS, :] = up[...].T
    out[2 * UNITS :, :] = down[...]


def stack_mlp(gate, up, down, after=()):
    return call(
        stack_kernel,
        [VMEM] * 3,
        [(shape(3 * UNITS, 128), VMEM)],
        [],
        [gate, up, down],
        after=after,
    )[0]


def copy_kernel(value, out):
    out[...] = value[...]


def copied(value, after):
    return call(copy_kernel, [VMEM], [(shape(*value.shape, dtype=value.dtype), VMEM)], [], [value], after=after)[0]


def row_kernel(*refs):
    for k in range(4):
        refs[4][k] = refs[k][...]


def stacked(parts, after):
    out = shape(4, *parts[0].shape)
    return call(row_kernel, [VMEM] * 4, [(out, VMEM)], [], parts, after=after)[0]


def norm_kernel(stream, gain, out):
    x = stream[...].astype(f32)
    inverse = lax.rsqrt(jnp.mean(x * x, axis=-1, keepdims=True) + epsilon)
    out[...] = (x * inverse * gain[...]).astype(bf16)


def normed(stream, gain, after):
    return call(
        norm_kernel, [VMEM] * 2, [(shape(BLOCK, D), VMEM)], [], [stream, gain[None]], after=after
    )[0]


def swap_bits(value, axes, change, name):
    sizes = [SIZES[a] for a in axes]
    pairs = []
    for index in np.ndindex(*sizes):
        pairs.append(
            (
                int(np.ravel_multi_index(index, sizes)),
                int(np.ravel_multi_index(change(*index), sizes)),
            )
        )
    with jax.named_scope(name):
        return lax.ppermute(value, axes if len(axes) > 1 else axes[0], pairs)


def over_z(value, k):
    return swap_bits(value, ("z",), lambda z: (z ^ k,), f"over_z{k}")


def over_x(value, k):
    return swap_bits(value, ("x",), lambda x: (x ^ k,), f"over_x{k}")


def over_y(value, k):
    return swap_bits(value, ("ylo", "yhi"), lambda lo, hi: (lo ^ (k & 1), hi ^ (k >> 1)), f"over_y{k}")


def over_core(value):
    return swap_bits(value, ("core",), lambda c: (c ^ 1,), "over_core")


def exchange(value):
    return swap_bits(value, ("core", "yhi"), lambda c, h: (h, c), "exchange")


def across(value, k, first):
    def change(x, lo, core, hi):
        if (core == 0) == first:
            return (x ^ k, lo, core, hi)
        return (x, lo ^ (k & 1), core, hi ^ (k >> 1))

    return swap_bits(value, ("x", "ylo", "core", "yhi"), change, f"across{k}" if first else f"second{k}")


def gather_pieces(parts, after):
    row = stacked(parts, after)
    own = [row] + [across(row, k, False) for k in (1, 2, 3)]
    return own + [over_core(v) for v in own]


def second_step(parts):
    return [parts[0]] + [across(parts[k], k, False) for k in (1, 2, 3)]


def first_step(parts):
    out = parts[0]
    for k in (1, 2, 3):
        out = out + across(parts[k], k, True).astype(f32)
    return out


def gather_tokens(value):
    return [value] + [over_z(value, k) for k in (1, 2, 3)]


def scatter_tokens(blocks):
    out = blocks[0]
    for k in (1, 2, 3):
        out = out + over_z(blocks[k], k).astype(f32)
    return out


def norm_forward(stream, gain):
    inverse = lax.rsqrt(jnp.mean(stream * stream, axis=-1, keepdims=True) + epsilon)
    return (stream * inverse * gain).astype(bf16), inverse


def body(
    block_input,
    segments,
    positions,
    attn_gain,
    w_query,
    w_key,
    w_value,
    w_output,
    mlp_gain,
    w_gate,
    w_up,
    w_down,
    cotangent,
):
    at_x, at_ylo, at_core, at_yhi, at_z = (lax.axis_index(a).astype(jnp.int32) for a in AXES)

    place = []
    for other in range(2):
        source = at_core ^ other
        for j in range(4):
            for i in range(4):
                dx = jnp.where(source == 0, i, j)
                dy = jnp.where(source == 0, j, i)
                place.append(at_yhi ^ (dy >> 1))
                place.append((at_x ^ dx) * 4 + (at_ylo ^ (dy & 1)) * 2 + source)
    zero = jnp.zeros((), jnp.int32)
    info = jnp.stack([at_core, at_z, at_x, at_ylo, at_yhi, zero, zero, zero] + place)

    piece = jnp.concatenate([w_query.T, w_key.T, w_value.T, w_output], axis=0)
    low_input = exchange(block_input.astype(bf16))
    grad_low = exchange(cotangent.astype(bf16))
    parts = [piece] + [across(piece, k, True) for k in (1, 2, 3)]
    act1 = normed(low_input, attn_gain, [*parts[1:], grad_low])
    act1_all = lax.all_gather(act1, "z", tiled=True)
    pieces = gather_pieces(parts, [act1])
    cot_all = gather_tokens(grad_low)
    piece_mlp = copied(
        stack_mlp(w_gate, w_up, w_down), [*pieces[1:4], act1_all, cot_all[1], cot_all[3]]
    )
    weights_mlp = lax.all_gather(piece_mlp, ("x", "ylo", "yhi", "core"))

    tables = jnp.stack([segments, positions])
    tables = jnp.where(at_core == at_yhi, tables, over_core(tables))
    segs, pos = tables[0], tables[1]
    seg_col, seg_row = segs[:, None], segs[None, :]
    frequency = base_freq ** (-(2.0 * jnp.arange(HEAD_DIM // 2, dtype=f32)) / HEAD_DIM)
    angles = pos.astype(f32)[:, None] * frequency[None, :]
    cosine, sine = jnp.cos(angles), jnp.sin(angles)
    cosine = jnp.concatenate([cosine, cosine], axis=1)
    sine = jnp.concatenate([-sine, sine], axis=1)

    def own_rows(table):
        return lax.dynamic_slice_in_dim(table, at_core * 512, 512, axis=0)

    keep, *away = project_qkv(info, act1_all, pieces, own_rows(cosine), own_rows(sine))
    qkv_mine, qkv_got = keep, [over_core(v) for v in away]
    keep, away = attend(info, qkv_mine, qkv_got, seg_col, seg_row, after=cot_all[2:3])
    att_mine, att_got = keep, over_core(away)
    blocks = project_out(info, att_mine, att_got, pieces)
    stream = low_input.astype(f32)
    inverse1 = lax.rsqrt(jnp.mean(stream * stream, axis=-1, keepdims=True) + epsilon)
    middle = stream + scatter_tokens(blocks)
    act2, inverse2 = norm_forward(middle, mlp_gain)
    act2_all = gather_tokens(act2)

    hid, gate_grad, up_grad, partial = mlp(info, act2_all, cot_all, weights_mlp)
    grad_act2 = lax.psum_scatter(partial, "z", tiled=True)
    away = mlp_away(info, hid, gate_grad, up_grad, act2_all, cot_all)
    got = over_core(away)
    (down,) = project_down(hid, weights_mlp, after=[away])
    parts = mlp_here(info, hid, gate_grad, up_grad, act2_all, cot_all, got, after=[down])
    grad_middle, middle_low, gain2_part = middle_back(
        middle, mlp_gain, grad_act2, grad_low, parts
    )
    mid_all = lax.all_gather(middle_low, "z", tiled=True)
    parts = second_step(parts)
    keep, away = project_out_back(info, mid_all, pieces, after=[parts[1], parts[3]])
    down = lax.psum_scatter(copied(down.reshape(512, D), [keep]), "z", tiled=True)
    out_block = exchange((middle + down.astype(f32)).astype(bf16))
    keep, away = attend_back(
        info, qkv_mine, qkv_got, keep, over_core(away), seg_col, seg_row, cosine, sine
    )
    g_mine, g_got = keep, over_core(away)
    parts = second_sum(parts, after=[g_mine])
    parts = [parts[0]] + [across(parts[k], k, True) for k in (1, 2, 3)]
    operands = [g_mine, g_got, att_mine, att_got, act1_all, mid_all]
    away = attn_away(info, operands, after=[parts[0]])
    partial, gain1_part = project_qkv_back(info, g_mine, g_got, pieces, act1_all, after=[away])
    grad_act1 = lax.psum_scatter(partial, "z", tiled=True)
    got = over_core(away)
    grad_mlp = parts[0] + sum(p.astype(f32) for p in parts[1:])
    parts = attn_here(info, operands, got, after=[*parts[1:], gain1_part, out_block])
    grad_input = input_back(low_input, attn_gain, grad_act1, grad_middle)
    grad_attn = first_step(second_sum(second_step(parts), after=[grad_input]))
    grad_input = exchange(grad_input).astype(f32)

    gains = jnp.concatenate([gain1_part / attn_gain, gain2_part])
    for step in (over_z, over_x, over_y):
        for k in (1, 2):
            gains = gains + step(gains, k)
    gains = gains + over_core(gains)
    w, n = WIDTH, UNITS
    return (
        out_block.astype(f32),
        grad_input,
        gains[0],
        grad_attn[:w].T,
        grad_attn[w : 2 * w].T,
        grad_attn[2 * w : 3 * w].T,
        grad_attn[3 * w :],
        gains[1],
        grad_mlp[:n].T,
        grad_mlp[n : 2 * n].T,
        grad_mlp[2 * n :],
    )


def solution(mesh):
    inner = Mesh(np.asarray(mesh.devices).reshape([SIZES[a] for a in AXES]), AXES)
    dp, tensor = ("x", "ylo", "core"), ("yhi", "z")
    rows, wide, tall = P(dp + tensor, None), P(dp, tensor), P(tensor, dp)
    return jax.shard_map(
        body,
        mesh=inner,
        in_specs=(
            rows, P(dp), P(dp), P(), wide, wide, wide, tall, P(), wide, wide, tall, rows,
        ),
        out_specs=(rows, rows, P(), wide, wide, wide, tall, P(), wide, wide, tall),
        check_vma=False,
    )
```

```python
import functools

import jax
import jax.numpy as jnp
import numpy as np
from jax import lax
from jax.experimental import pallas as pl
from jax.experimental.pallas import tpu as pltpu
from jax.sharding import Mesh, PartitionSpec as P

HEAD_DIM = 128
BLOCK = 128
D = 2048
UNITS = 688
WIDTH = 256
epsilon = 1e-05
base_freq = 10000.0
AXES = ("x", "ylo", "core", "yhi", "z")
SIZES = {"x": 4, "ylo": 2, "core": 2, "yhi": 2, "z": 4}
bf16 = jnp.bfloat16
f32 = jnp.float32
MIB = 1 << 20
VMEM = pl.BlockSpec(memory_space=pltpu.VMEM)
SMEM = pl.BlockSpec(memory_space=pltpu.SMEM)
ANY = pl.BlockSpec(memory_space=pl.ANY)
TOTAL = pltpu.VMEM((512, D), f32)
ROWS = pltpu.VMEM((512, D), bf16)
HALF = pltpu.VMEM((512, D // 2), bf16)


def dot_nn(a, b):
    return lax.dot_general(a, b, (((1,), (0,)), ((), ())), preferred_element_type=f32)


def dot_nt(a, b):
    return lax.dot_general(a, b, (((1,), (1,)), ((), ())), preferred_element_type=f32)


def dot_tn(a, b):
    return lax.dot_general(a, b, (((0,), (0,)), ((), ())), preferred_element_type=f32)


LOAD, STORE = "load", "store"


class Loaded:
    def __init__(self, source, target, sem):
        self.copy, self.target, self.here = pltpu.make_async_copy(source, target, sem), target, False
        self.copy.start()

    def get(self):
        if not self.here:
            self.copy.wait()
            self.here = True
        return self.target


class Stored:
    def __init__(self, target, source, sem):
        self.target, self.ref, self.sem, self.sent = target, source, sem, []

    def send(self, index=None):
        source, target = self.ref, self.target
        if index is not None:
            source, target = source.at[index], target.at[index]
        self.sent.append(pltpu.make_async_copy(source, target, self.sem))
        self.sent[-1].start()

    def finish(self):
        for copy in self.sent:
            copy.wait()


def call(kernel, ins, outs, scratch, operands, after=(), aliases=None, limit=62, cost=10**11):
    n_in, skip, n_out, n_scratch = len(operands), len(after), len(outs), len(scratch)
    scratch = list(scratch)
    for x, spec in [*zip(operands, ins), *outs]:
        if spec in (LOAD, STORE):
            scratch += [pltpu.VMEM(x.shape, x.dtype), pltpu.SemaphoreType.DMA]

    def run(*refs):
        given, results = list(refs[:n_in]), list(refs[n_in + skip : n_in + skip + n_out])
        rest = refs[n_in + skip + n_out :]
        own, extra = rest[:n_scratch], list(rest[n_scratch:])
        for k, spec in enumerate(ins):
            if spec == LOAD:
                given[k] = Loaded(given[k], extra.pop(0), extra.pop(0))
        for k, (_, spec) in enumerate(outs):
            if spec == STORE:
                results[k] = Stored(results[k], extra.pop(0), extra.pop(0))
        kernel(*given, *results, *own)
        for k, (_, spec) in enumerate(outs):
            if spec == STORE:
                results[k].finish()

    base = kernel.func if isinstance(kernel, functools.partial) else kernel
    suffix = str(kernel.args[0]) if isinstance(kernel, functools.partial) else ""
    name = base.__name__.strip("<>").replace("_kernel", "") + suffix

    def place(spec):
        return ANY if spec in (LOAD, STORE) else spec

    return pl.pallas_call(
        run,
        name=name,
        in_specs=[place(spec) for spec in ins] + [ANY] * skip,
        out_specs=[place(o[1]) for o in outs],
        out_shape=[o[0] for o in outs],
        scratch_shapes=scratch,
        input_output_aliases=aliases or {},
        compiler_params=pltpu.CompilerParams(vmem_limit_bytes=limit * MIB),
        cost_estimate=pl.CostEstimate(flops=cost, bytes_accessed=1000, transcendentals=0),
    )(*operands, *after)


def shape(*dims, dtype=bf16):
    return jax.ShapeDtypeStruct(dims, dtype)


def load_pieces(place, pieces, target, first, rows, sem):
    for j in range(8):
        for i in range(4):
            at = place[2 * (4 * j + i)]
            lane = pl.multiple_of(place[2 * (4 * j + i) + 1] * 128, 128)
            pltpu.make_async_copy(
                pieces[j].at[i, pl.ds(first, rows), :],
                target.at[at, :, pl.ds(lane, 128)],
                sem,
            ).start()


def fill(info, blocks, target):
    for k in range(4):
        at = pl.multiple_of((info[1] ^ k) * BLOCK, BLOCK)
        target[pl.ds(at, BLOCK), :] = blocks[k][...]


def wait_all(target, sem):
    pltpu.make_async_copy(target, target, sem).wait()


def fetch(info, blocks, target, sem):
    for k in range(4):
        at = pl.multiple_of((info[1] ^ k) * BLOCK, BLOCK)
        pltpu.make_async_copy(blocks[k], target.at[pl.ds(at, BLOCK), :], sem).start()


def qkv_kernel(info, *refs):
    acts, pieces = refs[:4], refs[4:12]
    cosine, sine, keep, away, weight, act, sems = *refs[12:15], refs[15:18], *refs[18:]
    core = info[0]
    fetch(info, acts, act, sems.at[0])
    load_pieces(info.at[pl.ds(8, 64)], pieces, weight, 0, 768, sems.at[1])
    wait_all(act, sems.at[0])
    wait_all(weight, sems.at[1])
    cosine, sine = cosine.get(), sine.get()
    for which, out in ((1, away), (0, keep)):
        s = core ^ which
        for m in range(3):
            got = dot_nt(act[...], weight[s, pl.ds(WIDTH * m, WIDTH), :])
            place = out.ref.at[m] if which == 0 else out[m].ref
            if m == 2:
                place[...] = got.astype(bf16)
            for h in range(2 if m < 2 else 0):
                v = got[:, HEAD_DIM * h : HEAD_DIM * h + HEAD_DIM]
                turned = pltpu.roll(v, HEAD_DIM // 2, 1)
                place[:, HEAD_DIM * h : HEAD_DIM * h + HEAD_DIM] = (
                    v * cosine[...] + turned * sine[...]
                ).astype(bf16)
            if which == 0:
                out.send(m)
            else:
                out[m].send()


def project_qkv(info, acts, pieces, cosine, sine, after=()):
    return call(
        qkv_kernel,
        [SMEM] + [ANY] * 12 + [LOAD] * 2,
        [(shape(3, 512, WIDTH), STORE)] + [(shape(512, WIDTH), STORE)] * 3,
        [pltpu.VMEM((2, 768, D), bf16), ROWS, pltpu.SemaphoreType.DMA((2,))],
        [info, *acts, *pieces, cosine, sine],
        cost=1000,
        after=after,
    )


TILE = 256


def masked_scores(q, k, seg_col, seg_row, first, count):
    s = dot_nt(q, k) * HEAD_DIM**-0.5
    rows = first + lax.broadcasted_iota(jnp.int32, (TILE, count), 0)
    cols = lax.broadcasted_iota(jnp.int32, (TILE, count), 1)
    ok = (cols <= rows) & (seg_col == seg_row)
    return jnp.where(ok, s, -1e30)


def softmax(s):
    e = jnp.exp(s - jnp.max(s, axis=-1, keepdims=True))
    return e * (1.0 / jnp.sum(e, axis=-1, keepdims=True))


def to_order(info, mine, got, target, m):
    for h, source in ((0, mine.at[m]), (1, got)):
        at = pl.multiple_of((info[0] ^ h) * 512, 512)
        target[m, pl.ds(at, 512), :] = source[...]


def from_order(info, source, m, target, h):
    at = pl.multiple_of((info[0] ^ h) * 512, 512)
    target[m] = source[m, pl.ds(at, 512), :]


def attend_kernel(info, mine, *refs):
    got, (seg_col, seg_row, keep, away, qkv, result) = refs[:3], refs[3:]
    for m in range(3):
        to_order(info, mine, got[m], qkv, m)
    for h in range(2):
        lanes = slice(HEAD_DIM * h, HEAD_DIM * h + HEAD_DIM)
        for t in range(1024 // TILE):
            n = TILE * (t + 1)
            rows = slice(TILE * t, n)
            s = masked_scores(
                qkv[0, rows, lanes], qkv[1, :n, lanes], seg_col[rows, :], seg_row[:, :n],
                TILE * t, n,
            )
            result[0, rows, lanes] = dot_nn(softmax(s).astype(bf16), qkv[2, :n, lanes]).astype(bf16)
    from_order(info, result, 0, away, 1)
    from_order(info, result, 0, keep, 0)


def attend(info, mine, got, seg_col, seg_row, after=()):
    return call(
        attend_kernel,
        [SMEM] + [VMEM] * 6,
        [(shape(1, 512, WIDTH), VMEM)] * 2,
        [pltpu.VMEM((3, 1024, WIDTH), bf16), pltpu.VMEM((1, 1024, WIDTH), bf16)],
        [info, mine, *got, seg_col, seg_row],
        limit=20,
        cost=1000,
        after=after,
    )


def attend_back_kernel(info, mine, *refs):
    got, (g_mine, g_got, seg_col, seg_row, cosine, sine, keep, away) = refs[:3], refs[3:11]
    qkv, grad, total, result = refs[11:]
    scale = HEAD_DIM**-0.5
    for m in range(3):
        to_order(info, mine, got[m], qkv, m)
    to_order(info, g_mine, g_got.at[0], grad, 0)
    for h in range(2):
        lanes = slice(HEAD_DIM * h, HEAD_DIM * h + HEAD_DIM)
        total[...] = jnp.zeros_like(total)
        for t in range(1024 // TILE):
            n = TILE * (t + 1)
            rows = slice(TILE * t, n)
            q, g = qkv[0, rows, lanes], grad[0, rows, lanes]
            s = masked_scores(q, qkv[1, :n, lanes], seg_col[rows, :], seg_row[:, :n], TILE * t, n)
            p = softmax(s)
            dp = dot_nt(g, qkv[2, :n, lanes])
            ds = (p * (dp - jnp.sum(p * dp, axis=-1, keepdims=True))).astype(bf16)
            total[0, rows, :] = dot_nn(ds, qkv[1, :n, lanes]) * scale
            total[1, :n, :] += dot_tn(ds, q) * scale
            total[2, :n, :] += dot_tn(p.astype(bf16), g)
        for m in range(2):
            v = total[m]
            turned = pltpu.roll(v, HEAD_DIM // 2, 1)
            result[m, :, lanes] = (v * cosine[...] - turned * sine[...]).astype(bf16)
        result[2, :, lanes] = total[2].astype(bf16)
    for m in range(3):
        from_order(info, result, m, away, 1)
        from_order(info, result, m, keep, 0)


def attend_back(info, mine, got, g_mine, g_got, seg_col, seg_row, cosine, sine, after=()):
    return call(
        attend_back_kernel,
        [SMEM] + [VMEM] * 10,
        [(shape(3, 512, WIDTH), VMEM)] * 2,
        [
            pltpu.VMEM((3, 1024, WIDTH), bf16),
            pltpu.VMEM((1, 1024, WIDTH), bf16),
            pltpu.VMEM((3, 1024, HEAD_DIM), f32),
            pltpu.VMEM((3, 1024, WIDTH), bf16),
        ],
        [info, mine, *got, g_mine, g_got, seg_col, seg_row, cosine, sine],
        cost=1000,
        after=after,
    )


def write_blocks(info, total, outs):
    for k in range(4):
        at = pl.multiple_of((info[1] ^ k) * BLOCK, BLOCK)
        outs[k][...] = total[pl.ds(at, BLOCK), :].astype(outs[k].dtype)


BLOCK_OUTS = [(shape(BLOCK, D, dtype=f32), VMEM)] + [(shape(BLOCK, D), VMEM)] * 3


def out_kernel(info, mine, got, *refs):
    pieces, outs, (weight, total, sem) = refs[:8], refs[8:12], refs[12:]
    core = info[0]
    load_pieces(info.at[pl.ds(8, 64)], pieces, weight, 768, 256, sem)
    mine, got = mine.get(), got.get()
    wait_all(weight, sem)
    total[...] = dot_nn(mine[0], weight[core]) + dot_nn(got[0], weight[core ^ 1])
    write_blocks(info, total, outs)


def project_out(info, mine, got, pieces, after=()):
    return call(
        out_kernel,
        [SMEM] + [LOAD] * 2 + [ANY] * 8,
        BLOCK_OUTS,
        [pltpu.VMEM((2, 256, D), bf16), TOTAL, pltpu.SemaphoreType.DMA],
        [info, mine, got, *pieces],
        limit=20,
        cost=1000,
        after=after,
    )


def out_back_kernel(info, *refs):
    act, pieces = refs[0], refs[1:9]
    keep, away, weight, sem = refs[9:]
    core = info[0]
    load_pieces(info.at[pl.ds(8, 64)], pieces, weight, 768, 256, sem)
    act = act.get()
    wait_all(weight, sem)
    for which, out in ((1, away), (0, keep)):
        out.ref[0] = dot_nt(act[...], weight[core ^ which]).astype(bf16)
        out.send()


def project_out_back(info, act, pieces, after=()):
    return call(
        out_back_kernel,
        [SMEM] + [LOAD] + [ANY] * 8,
        [(shape(1, 512, WIDTH), STORE)] * 2,
        [pltpu.VMEM((2, 256, D), bf16), pltpu.SemaphoreType.DMA],
        [info, act, *pieces],
        after=after,
    )


def qkv_back_kernel(info, mine, got, *refs):
    pieces, acts = refs[:8], refs[8:12]
    out, gain, weight, total, act, sem, act_sem = refs[12:]
    fetch(info, acts, act, act_sem)
    core = info[0]
    load_pieces(info.at[pl.ds(8, 64)], pieces, weight, 0, 768, sem)
    wait_all(weight, sem)
    mine, got = mine.get(), got.get()
    for which, source in ((0, mine), (1, got)):
        for m in range(3):
            part = dot_nn(source[m], weight[core ^ which, pl.ds(WIDTH * m, WIDTH), :])
            if which == 0 and m == 0:
                total[...] = part
            else:
                total[...] += part
    out.ref[...] = total[...].astype(bf16)
    out.send()
    wait_all(act, act_sem)
    gain[...] = jnp.sum(total[...] * act[...].astype(f32), axis=0, keepdims=True)


def project_qkv_back(info, mine, got, pieces, acts, after=()):
    return call(
        qkv_back_kernel,
        [SMEM] + [LOAD] * 2 + [ANY] * 12,
        [(shape(512, D), STORE), (shape(1, D, dtype=f32), VMEM)],
        [pltpu.VMEM((2, 768, D), bf16), TOTAL, ROWS]
        + [pltpu.SemaphoreType.DMA] * 2,
        [info, mine, got, *pieces, *acts],
        after=after,
    )


def load_gathered(weights, target, s, first, rows, row, sem):
    for x in range(4):
        for y in range(2):
            for c in range(2):
                f = x * 4 + y * 2 + c
                pltpu.make_async_copy(
                    weights.at[x * 8 + y * 4 + s * 2 + c, pl.ds(first, rows), :],
                    target.at[s, pl.ds(row, rows), f * 128 : f * 128 + 128],
                    sem,
                ).start()


def mlp_kernel(info, *refs):
    acts, cots, weights = refs[:4], refs[4:8], refs[8]
    hid, gate_grad, up_grad = refs[9:12]
    outs = refs[12:16]
    weight, act, cot, total, sems = refs[16:]
    n = UNITS
    fetch(info, acts, act, sems.at[3])
    load_gathered(weights, weight, 0, 0, n, 0, sems.at[0])
    load_gathered(weights, weight, 0, n, 2 * n, n, sems.at[1])
    fetch(info, cots, cot, sems.at[4])
    wait_all(act, sems.at[3])
    for s in range(2):
        if s == 0:
            wait_all(weight.at[0, pl.ds(0, n), :], sems.at[0])
        else:
            wait_all(weight.at[1], sems.at[2])
        gate = dot_nt(act[...], weight[s, pl.ds(0, n), :])
        if s == 0:
            load_gathered(weights, weight, 1, 0, 3 * n, 0, sems.at[2])
            wait_all(weight.at[0, pl.ds(n, 2 * n), :], sems.at[1])
            wait_all(cot, sems.at[4])
        up = dot_nt(act[...], weight[s, pl.ds(n, n), :])
        hg = dot_nt(cot[...], weight[s, pl.ds(2 * n, n), :])
        sig = 1.0 / (1.0 + jnp.exp(-gate))
        silu = gate * sig
        hid.ref[s] = (silu * up).astype(bf16)
        gate_grad.ref[s] = (hg * up * (sig * (1.0 + gate * (1.0 - sig)))).astype(bf16)
        up_grad.ref[s] = (hg * silu).astype(bf16)
        for result in (hid, gate_grad, up_grad):
            result.send(s)
        part = dot_nn(gate_grad.ref[s], weight[s, pl.ds(0, n), :]) + dot_nn(
            up_grad.ref[s], weight[s, pl.ds(n, n), :]
        )
        if s == 0:
            total[...] = part
        else:
            total[...] += part
    for k in (2, 1, 3, 0):
        at = pl.multiple_of((info[1] ^ k) * BLOCK, BLOCK)
        outs[k].ref[...] = total[pl.ds(at, BLOCK), :].astype(outs[k].ref.dtype)
        outs[k].send()


def mlp(info, acts, cots, weights, after=()):
    return call(
        mlp_kernel,
        [SMEM] + [ANY] * 9,
        [(shape(2, 512, UNITS), STORE)] * 3
        + [(shape(BLOCK, D, dtype=f32), STORE)]
        + [(shape(BLOCK, D), STORE)] * 3,
        [pltpu.VMEM((2, 3 * UNITS, D), bf16), ROWS, ROWS, TOTAL, pltpu.SemaphoreType.DMA((5,))],
        [info, *acts, *cots, weights],
        after=after,
    )


def down_kernel(hid, weights, out, weight, total, sems):
    for s in range(2):
        load_gathered(weights, weight, s, 2 * UNITS, UNITS, 0, sems.at[s])
    hid = hid.get()
    wait_all(weight.at[0], sems.at[0])
    total[...] = dot_nn(hid[0], weight[0])
    wait_all(weight.at[1], sems.at[1])
    out.ref[...] = (total[...] + dot_nn(hid[1], weight[1])).astype(bf16)
    out.send()


def project_down(hid, weights, after=()):
    return call(
        down_kernel,
        [LOAD, ANY],
        [(shape(512, D), STORE)],
        [pltpu.VMEM((2, UNITS, D), bf16), TOTAL, pltpu.SemaphoreType.DMA((2,))],
        [hid, weights],
        after=after,
    )


def half_features(info, source, target, which):
    core, x, y = info[0], info[2], info[3]
    for dx in range(4):
        for dlo in range(2):
            lane = ((x ^ dx) * 4 + (y ^ dlo) * 2 + (core ^ which)) * 128
            b = 2 * dx + dlo
            target[:, 128 * b : 128 * b + 128] = source[:, pl.ds(pl.multiple_of(lane, 128), 128)]


class Joined:
    def __init__(self, ref):
        self.ref = ref

    def __getitem__(self, j):
        return self.ref.at[j]


def send_blocks(on_core, stage, slot, outs, rows, h, sem):
    def send(c):
        for dx in range(4):
            for dlo in range(2):
                dy = dlo + 2 * h
                i, j = (dx, dy) if c == 0 else (dy, dx)
                pltpu.make_async_copy(
                    stage.at[slot, 2 * dx + dlo], outs[j].at[i, rows, :], sem
                ).start()

    pl.when(on_core == 0)(functools.partial(send, 0))
    pl.when(on_core == 1)(functools.partial(send, 1))


def half_grads(on_core, lefts, rights, units, outs, stage, sems, got=None):
    step = 0
    for m in range(len(rights)):
        right = rights[m]()
        rows = pl.ds(units * m, units)
        for h in range(2):
            slot = step % 2
            part = dot_tn(lefts(h, m), right[...])
            if step >= 2:
                wait_all(stage.at[slot], sems.at[slot])
            more = got(m) if got else None
            for dx in range(4):
                for dlo in range(2):
                    b, dy = 2 * dx + dlo, dlo + 2 * h
                    block = part[:, 128 * b : 128 * b + 128]
                    if got:
                        i = jnp.where(on_core == 0, dx, dy)
                        j = jnp.where(on_core == 0, dy, dx)
                        block = block + more[j, i, rows, :].astype(f32)
                    stage[slot, b] = block.astype(bf16)
            send_blocks(on_core, stage, slot, outs, rows, h, sems.at[slot])
            step += 1
    for slot in range(2):
        wait_all(stage.at[slot], sems.at[slot])


def load_got(pieces, target, units, sems, count):
    for m in range(count):
        for j in range(4):
            rows = pl.ds(units * m, units)
            pltpu.make_async_copy(
                pieces[j].at[:, rows, :], target.at[j, :, rows, :], sems.at[m]
            ).start()
    waited = []

    def got(m):
        if m not in waited:
            waited.append(m)
            part = target.at[:, :, pl.ds(units * m, units), :]
            pltpu.make_async_copy(part, part, sems.at[m]).wait()
        return target

    return got


def mlp_rights(info, acts, cots, act, cot, act_half, cot_half, sems, which):
    fetch(info, acts, act, sems.at[0])
    fetch(info, cots, cot, sems.at[1])

    def first():
        wait_all(act, sems.at[0])
        half_features(info, act, act_half, which)
        return act_half

    def last():
        wait_all(cot, sems.at[1])
        half_features(info, cot, cot_half, which)
        return cot_half

    return first, lambda: act_half, last


def mlp_grads_kernel(which, info, gate_grad, up_grad, hid, *refs):
    acts, cots, refs = refs[:4], refs[4:8], refs[8:]
    got = None
    if which == 0:
        piece, outs, refs = Joined(refs[0]), refs[2:6], refs[7:]
    else:
        outs, refs = Joined(refs[0]), refs[1:]
    act, cot, act_half, cot_half, stage, sems, in_sems = refs[:7]
    rights = mlp_rights(info, acts, cots, act, cot, act_half, cot_half, in_sems, which)
    if which == 0:
        got = load_got(piece, refs[7], UNITS, refs[8], 3)
    sources = (gate_grad, up_grad, hid)
    half_grads(
        info[0] ^ which, lambda h, m: sources[m].get()[info[4] ^ h], rights, UNITS, outs,
        stage, sems, got,
    )


def mlp_grads(which, info, hid, gate_grad, up_grad, acts, cots, got=(), passed=(), after=()):
    scratch = [
        ROWS, ROWS, HALF, HALF, pltpu.VMEM((2, 8, UNITS, 128), bf16),
        pltpu.SemaphoreType.DMA((2,)), pltpu.SemaphoreType.DMA((2,)),
    ]
    if which == 0:
        scratch += [pltpu.VMEM((4, 4, 3 * UNITS, 128), bf16), pltpu.SemaphoreType.DMA((3,))]
    return call(
        functools.partial(mlp_grads_kernel, which),
        [SMEM] + [LOAD] * 3 + [ANY] * (8 + len(got) + len(passed)),
        [(shape(4, 3 * UNITS, 128), ANY)] * 4 + [(shape(*v.shape), ANY) for v in passed]
        if which == 0 else [(shape(4, 4, 3 * UNITS, 128), ANY)],
        scratch,
        [info, gate_grad, up_grad, hid, *acts, *cots, *got, *passed],
        after=after,
        aliases={13: 4} if passed else None,
    )


def split_gains(gains, total, halves):
    for b in range(16):
        lanes = slice(128 * b, 128 * b + 128)
        total[b : b + 1, :] = gains[0:1, lanes]
        total[16 + b : 17 + b, :] = gains[1:2, lanes]
    coarse = total[...].astype(bf16)
    halves[0:32, :] = coarse
    halves[32:64, :] = (total[...] - coarse.astype(f32)).astype(bf16)


def attn_grads_kernel(which, info, mine, got_heads, att_mine, att_got, mid, *refs):
    acts, refs = refs[:4], refs[4:]
    got = None
    if which == 0:
        piece, gains, outs, refs = Joined(refs[0]), refs[1], refs[2:6], refs[6:]
        split_gains(gains, *refs[9:11])
        for j in range(4):
            for i in range(4):
                pltpu.make_async_copy(
                    refs[10].at[pl.ds(16 * i, 16), :],
                    outs[j].at[i, pl.ds(4 * WIDTH, 16), :],
                    refs[11],
                ).start()
    else:
        outs, refs = Joined(refs[0]), refs[1:]
    left, act_half, mid_half, stage, sems, act, act_sem = refs[:7]
    fetch(info, acts, act, act_sem)
    if which == 0:
        got = load_got(piece, refs[7], WIDTH, refs[8], 4)
    for w, (grads, att) in enumerate(((mine, att_mine), (got_heads, att_got))):
        left[w, 0:3] = grads.get()[...]
        left[w, 3] = att.get()[0]

    def first():
        wait_all(act, act_sem)
        half_features(info, act, act_half, which)
        return act_half

    def last():
        half_features(info, mid.get(), mid_half, which)
        return mid_half

    half_grads(
        info[0] ^ which, lambda h, m: left[info[0] ^ info[4] ^ h, m],
        (first, lambda: act_half, lambda: act_half, last), WIDTH, outs, stage, sems, got,
    )
    if which == 0:
        for j in range(4):
            wait_all(refs[10], refs[11])


def attn_grads(which, info, operands, got=(), gains=(), after=()):
    scratch = [
        pltpu.VMEM((2, 4, 512, WIDTH), bf16), HALF, HALF,
        pltpu.VMEM((2, 8, WIDTH, 128), bf16), pltpu.SemaphoreType.DMA((2,)),
        ROWS, pltpu.SemaphoreType.DMA,
    ]
    if which == 0:
        scratch += [
            pltpu.VMEM((4, 4, 4 * WIDTH, 128), bf16), pltpu.SemaphoreType.DMA((4,)),
            pltpu.VMEM((32, 128), f32), pltpu.VMEM((64, 128), bf16), pltpu.SemaphoreType.DMA,
        ]
    return call(
        functools.partial(attn_grads_kernel, which),
        [SMEM] + [LOAD] * 5 + [ANY] * (4 + len(got)) + [VMEM] * len(gains),
        [(shape(4, 4 * WIDTH + 16, 128), ANY)] * 4 if which == 0 else
        [(shape(4, 4, 4 * WIDTH, 128), ANY)],
        scratch,
        [info, *operands, *got, *gains],
        cost=10**11 if which == 0 else 1000,
        after=after,
    )


def norm_back(x, gain, gradient):
    inverse = lax.rsqrt(jnp.mean(x * x, axis=-1, keepdims=True) + epsilon)
    scaled = gradient * gain
    mean_term = jnp.mean(scaled * x, axis=-1, keepdims=True)
    back = inverse * scaled - x * (inverse * inverse * inverse) * mean_term
    return back, inverse


def middle_back_kernel(middle, gain, cotangent, *refs):
    gradient, (out, low, gain_part) = refs[:4], refs[4:]
    x, e = middle[...], gradient[0][...]
    for v in gradient[1:]:
        e = e + v[...].astype(f32)
    back, inverse = norm_back(x, gain[...], e)
    total = cotangent[...].astype(f32) + back
    out[...] = total
    low[...] = total.astype(bf16)
    gain_part[...] = jnp.sum(e * x * inverse, axis=0, keepdims=True)


def middle_back(middle, gain, gradient, cotangent, after):
    return call(
        middle_back_kernel,
        [VMEM] * 7,
        [
            (shape(BLOCK, D, dtype=f32), VMEM),
            (shape(BLOCK, D), VMEM),
            (shape(1, D, dtype=f32), VMEM),
        ],
        [],
        [middle, gain[None], cotangent, *gradient],
        after=after,
    )


def input_back_kernel(stream, gain, gradient, middle, out):
    back, _ = norm_back(stream[0:BLOCK, :].astype(f32), gain[...], gradient[...].astype(f32))
    out[...] = (middle[...] + back).astype(bf16)


def input_back(stream, gain, gradient, middle, after):
    return call(
        input_back_kernel,
        [VMEM] * 4,
        [(shape(BLOCK, D), VMEM)],
        [],
        [stream, gain[None], gradient, middle],
        after=after,
    )[0]


def second_sum(parts, gains=False, after=()):
    rows = parts[0].shape[1] - 16 * gains
    more = 64 * gains

    def second_sum_kernel(*refs):
        ins, outs = [r.get() for r in refs[:4]], refs[4:]
        if gains:
            low = pl.ds(rows, 16)
            part = []
            for v in ins:
                coarse = jnp.concatenate([v[0, low, :], v[1, low, :]], axis=0)
                fine = jnp.concatenate([v[2, low, :], v[3, low, :]], axis=0)
                part.append(coarse.astype(f32) + fine.astype(f32))
            total = (part[0] + part[1]) + (part[2] + part[3])
            coarse = total.astype(bf16)
            fine = (total - coarse.astype(f32)).astype(bf16)
        for k in (1, 2, 3, 0):
            out = outs[k].ref
            total = ins[0][k, 0:rows, :].astype(f32)
            for v in ins[1:]:
                total = total + v[k, 0:rows, :].astype(f32)
            out[0:rows, :] = total.astype(out.dtype)
            if gains:
                out[rows : rows + 32, :] = coarse.astype(out.dtype)
                out[rows + 32 :, :] = fine.astype(out.dtype)
            outs[k].send()

    return call(
        second_sum_kernel,
        [LOAD] * 4,
        [(shape(rows + more, 128, dtype=f32 if k == 0 else bf16), STORE) for k in range(4)],
        [],
        [*parts],
        after=after,
    )


def final_sum(parts, plan):
    def final_sum_kernel(*refs):
        ins, outs = refs[:4], refs[4:]
        for (first, rows, turn), out in zip(plan, outs):
            part = [v[first : first + rows, :].astype(f32) for v in ins]
            total = (part[0] + part[1]) + (part[2] + part[3])
            out[...] = total.T if turn else total

    outs = [
        (shape(*((128, rows) if turn else (rows, 128)), dtype=f32), VMEM)
        for _, rows, turn in plan
    ]
    return call(final_sum_kernel, [VMEM] * 4, outs, [], list(parts), limit=24, cost=1000)


def widen_kernel(value, out):
    out[...] = value[...].astype(f32)


def widen(value, after=()):
    return call(
        widen_kernel,
        [VMEM],
        [(shape(*value.shape, dtype=f32), VMEM)],
        [],
        [value],
        after=after,
        cost=1000,
    )[0]


def stack_attn_kernel(query, key, value, output, out):
    w = WIDTH
    for m, ref in enumerate((query, key, value)):
        out[w * m : w * m + w, :] = ref[...].T
    out[3 * w :, :] = output[...]


def stack_attn(query, key, value, output):
    return call(
        stack_attn_kernel,
        [VMEM] * 4,
        [(shape(4 * WIDTH, 128), VMEM)],
        [],
        [query, key, value, output],
        cost=1000,
    )[0]


def joined_kernel(stream, more, out):
    out[...] = (stream[...] + more[...].astype(f32)).astype(bf16)


def joined(stream, more, after):
    return call(
        joined_kernel,
        [VMEM] * 2,
        [(shape(BLOCK, D), VMEM)],
        [],
        [stream, more],
        after=after,
        cost=1000,
    )[0]


def stack_kernel(*refs):
    gate, up, down, out = refs[0], refs[1], refs[2], refs[-1]
    out[0:UNITS, :] = gate[...]
    out[UNITS : 2 * UNITS, :] = up[...]
    out[2 * UNITS :, :] = down[...]


def stack_mlp(gate, up, down, after=()):
    return call(
        stack_kernel,
        [VMEM] * 3,
        [(shape(3 * UNITS, 128), VMEM)],
        [],
        [gate, up, down],
        after=after,
    )[0]


def copy_kernel(value, out):
    out[...] = value[...]


def copied(value, after):
    return call(copy_kernel, [VMEM], [(shape(*value.shape, dtype=value.dtype), VMEM)], [], [value], after=after)[0]


def held_kernel(*refs):
    del refs


def held_all(values, after):
    return call(
        held_kernel,
        [ANY] * len(values),
        [(shape(*v.shape, dtype=v.dtype), ANY) for v in values],
        [],
        values,
        after=after,
        aliases={k: k for k in range(len(values))},
        cost=1000,
    )


def held(value, after):
    return held_all([value], after)[0]


def start_kernel(stream, gain, *refs):
    parts, out, row = refs[:4], refs[4], refs[5]
    for k in range(4):
        row.ref[k] = parts[k].get()[...]
        row.send(k)
    x = stream.get()[0:BLOCK, :].astype(f32)
    inverse = lax.rsqrt(jnp.mean(x * x, axis=-1, keepdims=True) + epsilon)
    out[...] = (x * inverse * gain[...]).astype(bf16)


def start(stream, gain, parts, after):
    return call(
        start_kernel,
        [LOAD, VMEM] + [LOAD] * 4,
        [(shape(BLOCK, D), VMEM), (shape(4, *parts[0].shape), STORE)],
        [],
        [stream, gain[None], *parts],
        after=after,
    )


def swap_bits(value, axes, change, name):
    sizes = [SIZES[a] for a in axes]
    pairs = []
    for index in np.ndindex(*sizes):
        pairs.append(
            (
                int(np.ravel_multi_index(index, sizes)),
                int(np.ravel_multi_index(change(*index), sizes)),
            )
        )
    with jax.named_scope(name):
        return lax.ppermute(value, axes if len(axes) > 1 else axes[0], pairs)


def over_z(value, k):
    return swap_bits(value, ("z",), lambda z: (z ^ k,), f"over_z{k}")


def over_x(value, k):
    return swap_bits(value, ("x",), lambda x: (x ^ k,), f"over_x{k}")


def over_y(value, k):
    return swap_bits(value, ("ylo", "yhi"), lambda lo, hi: (lo ^ (k & 1), hi ^ (k >> 1)), f"over_y{k}")


def over_core(value):
    return swap_bits(value, ("core",), lambda c: (c ^ 1,), "over_core")


def exchange(value):
    return swap_bits(value, ("core", "yhi"), lambda c, h: (h, c), "exchange")


def across(value, k, first):
    def change(x, lo, core, hi):
        if (core == 0) == first:
            return (x ^ k, lo, core, hi)
        return (x, lo ^ (k & 1), core, hi ^ (k >> 1))

    return swap_bits(value, ("x", "ylo", "core", "yhi"), change, f"across{k}" if first else f"second{k}")


def second_step(parts):
    return [parts[0]] + [across(parts[k], k, False) for k in (1, 2, 3)]


def first_step(parts):
    out = parts[0]
    for k in (1, 2, 3):
        out = out + across(parts[k], k, True).astype(f32)
    return out


def gather_tokens(value):
    return [value] + [over_z(value, k) for k in (1, 2, 3)]


def scatter_tokens(blocks):
    out = blocks[0]
    for k in (1, 2, 3):
        out = out + over_z(blocks[k], k).astype(f32)
    return out


def norm_forward(stream, gain):
    inverse = lax.rsqrt(jnp.mean(stream * stream, axis=-1, keepdims=True) + epsilon)
    return (stream * inverse * gain).astype(bf16), inverse


def body(
    block_input,
    segments,
    positions,
    attn_gain,
    w_query,
    w_key,
    w_value,
    w_output,
    mlp_gain,
    w_gate,
    w_up,
    w_down,
    cotangent,
):
    at_x, at_ylo, at_core, at_yhi, at_z = (lax.axis_index(a).astype(jnp.int32) for a in AXES)

    place = []
    for other in range(2):
        source = at_core ^ other
        for j in range(4):
            for i in range(4):
                dx = jnp.where(source == 0, i, j)
                dy = jnp.where(source == 0, j, i)
                place.append(at_yhi ^ (dy >> 1))
                place.append((at_x ^ dx) * 4 + (at_ylo ^ (dy & 1)) * 2 + source)
    zero = jnp.zeros((), jnp.int32)
    info = jnp.stack([at_core, at_z, at_x, at_ylo, at_yhi, zero, zero, zero] + place)

    extra = jnp.stack(
        [
            jnp.concatenate([positions // 64, positions % 64]),
            jnp.concatenate([segments, jnp.zeros_like(segments)]),
        ]
    ).astype(bf16)
    low_input = exchange(
        jnp.concatenate([block_input.astype(bf16), jnp.pad(extra, ((0, 14), (0, 0)))])
    )
    extra = low_input[BLOCK : BLOCK + 2].astype(f32)
    pos = extra[0, :1024] * 64.0 + extra[0, 1024:]
    segs = extra[1, :1024].astype(jnp.int32)
    seg_col, seg_row = segs[:, None], segs[None, :]
    frequency = base_freq ** (-(2.0 * jnp.arange(HEAD_DIM // 2, dtype=f32)) / HEAD_DIM)
    angles = pos[:, None] * frequency[None, :]
    cosine, sine = jnp.cos(angles), jnp.sin(angles)
    cosine = jnp.concatenate([cosine, cosine], axis=1)
    sine = jnp.concatenate([-sine, sine], axis=1)

    piece = stack_attn(w_query, w_key, w_value, w_output)
    grad_low = exchange(cotangent.astype(bf16))
    parts = [piece] + [across(piece, k, True) for k in (1, 2, 3)]
    act1, row = start(low_input, attn_gain, parts, [grad_low])
    act1_all = [act1, over_z(act1, 1), None, over_z(act1, 3)]
    pieces = [row, across(row, 1, False), None, across(row, 3, False)]
    act1_all[2] = over_z(held(act1, [act1_all[1], act1_all[3]]), 2)
    pieces[2] = across(row, 2, False)
    pieces = pieces + [over_core(v) for v in pieces]
    cot_all = gather_tokens(grad_low)
    def own_rows(table):
        return lax.dynamic_slice_in_dim(table, at_core * 512, 512, axis=0)

    tables = [own_rows(cosine), own_rows(sine)]
    piece_mlp = stack_mlp(w_gate.T, w_up.T, w_down, after=[cosine, sine, seg_col, *tables])
    piece_mlp = held(piece_mlp, [*pieces[1:4], act1_all[2]])
    weights_mlp = lax.all_gather(piece_mlp, ("x", "ylo", "yhi", "core"))

    keep, *away = project_qkv(info, act1_all, pieces, *tables, after=[piece_mlp])
    qkv_mine, qkv_got = keep, [over_core(v) for v in away]
    keep, away = attend(info, qkv_mine, qkv_got, seg_col, seg_row, after=[cot_all[1], cot_all[3]])
    att_mine, att_got = keep, over_core(away)
    blocks = project_out(info, att_mine, att_got, pieces, after=cot_all[2:3])
    stream = low_input[:BLOCK].astype(f32)
    inverse1 = lax.rsqrt(jnp.mean(stream * stream, axis=-1, keepdims=True) + epsilon)
    middle = stream + scatter_tokens(blocks)
    act2, inverse2 = norm_forward(middle, mlp_gain)
    act2_all = gather_tokens(act2)

    hid, gate_grad, up_grad, *blocks = mlp(info, act2_all, cot_all, weights_mlp)
    grad_act2 = [blocks[0]] + [over_z(blocks[k], k) for k in (1, 2, 3)]
    operands = [info, hid, gate_grad, up_grad, act2_all, cot_all]
    (away,) = mlp_grads(1, *operands)
    got = over_core(away)
    (down,) = project_down(hid, weights_mlp, after=[away])
    grad_middle, middle_low, gain2_part = middle_back(
        middle, mlp_gain, grad_act2, grad_low, [down, got]
    )
    mid_all = lax.all_gather(middle_low, "z", tiled=True)
    *parts, down = mlp_grads(0, *operands, [got], [down], after=[middle_low])
    first, third = across(parts[1], 1, False), across(parts[3], 3, False)
    keep, away = project_out_back(info, mid_all, pieces, after=parts[:1])
    second = held(parts[2], [keep, first, third])
    kept = second
    second = across(second, 2, False)
    parts = [parts[0], first, second, third]
    down = lax.psum_scatter(down, "z", tiled=True)
    keep, away = attend_back(
        info, qkv_mine, qkv_got, keep, over_core(away), seg_col, seg_row, cosine, sine,
        after=[kept],
    )
    g_mine, g_got = keep, over_core(away)
    operands = [g_mine, g_got, att_mine, att_got, mid_all, *act1_all]
    (away,) = attn_grads(1, info, operands)
    got = over_core(away)
    parts = second_sum(parts, after=[away])
    partial, gain1_part = project_qkv_back(
        info, g_mine, g_got, pieces, act1_all, after=[away, parts[0]]
    )
    out_block = exchange(joined(middle, down, [gain1_part]))
    grad_act1 = lax.psum_scatter(partial, "z", tiled=True)
    parts = [parts[0]] + [across(parts[k], k, True) for k in (1, 2, 3)]
    grad_gate, grad_up, grad_down = final_sum(
        parts, ((0, UNITS, False), (UNITS, UNITS, False), (2 * UNITS, UNITS, False))
    )
    gains = [jnp.concatenate([gain1_part / attn_gain, gain2_part])]
    outs = attn_grads(0, info, operands, [got], gains, after=parts[:1])
    grad_input = input_back(
        low_input, attn_gain, grad_act1, grad_middle, [outs[0], *parts[1:]]
    )
    out_block = widen(out_block, [grad_input])
    grad_input = widen(exchange(grad_input))
    parts = second_sum(second_step(outs), True, after=[grad_input, grad_down, out_block])
    parts = [parts[0]] + [across(parts[k], k, True) for k in (1, 2, 3)]
    w, n = WIDTH, UNITS
    grad_query, grad_key, grad_value, grad_output, coarse, fine = final_sum(
        parts,
        ((0, w, True), (w, w, True), (2 * w, w, True), (3 * w, w, False),
         (4 * w, 32, False), (4 * w + 32, 32, False)),
    )
    gains = (coarse + fine).reshape(2, D)
    one, two, three = (over_z(gains, k) for k in (1, 2, 3))
    gains = (gains + one) + (two + three)
    gains = gains + over_core(gains)
    return (
        out_block,
        grad_input,
        gains[0],
        grad_query,
        grad_key,
        grad_value,
        grad_output,
        gains[1],
        grad_gate.T,
        grad_up.T,
        grad_down,
    )


def solution(mesh):
    inner = Mesh(np.asarray(mesh.devices).reshape([SIZES[a] for a in AXES]), AXES)
    dp, tensor = ("x", "ylo", "core"), ("yhi", "z")
    rows, wide, tall = P(dp + tensor, None), P(dp, tensor), P(tensor, dp)
    return jax.shard_map(
        body,
        mesh=inner,
        in_specs=(
            rows, P(dp), P(dp), P(), wide, wide, wide, tall, P(), wide, wide, tall, rows,
        ),
        out_specs=(rows, rows, P(), wide, wide, wide, tall, P(), wide, wide, tall),
        check_vma=False,
    )
```

```python
import functools

import jax
import jax.numpy as jnp
import numpy as np
from jax import lax
from jax.experimental import pallas as pl
from jax.experimental.pallas import tpu as pltpu
from jax.sharding import Mesh, PartitionSpec as P

HEAD_DIM = 128
BLOCK = 128
D = 2048
UNITS = 688
WIDTH = 256
epsilon = 1e-05
base_freq = 10000.0
AXES = ("x", "ylo", "core", "yhi", "z")
SIZES = {"x": 4, "ylo": 2, "core": 2, "yhi": 2, "z": 4}
bf16 = jnp.bfloat16
f32 = jnp.float32
MIB = 1 << 20
VMEM = pl.BlockSpec(memory_space=pltpu.VMEM)
SMEM = pl.BlockSpec(memory_space=pltpu.SMEM)
ANY = pl.BlockSpec(memory_space=pl.ANY)
TOTAL = pltpu.VMEM((512, D), f32)
ROWS = pltpu.VMEM((512, D), bf16)
HALF = pltpu.VMEM((512, D // 2), bf16)


def dot_nn(a, b):
    return lax.dot_general(a, b, (((1,), (0,)), ((), ())), preferred_element_type=f32)


def dot_nt(a, b):
    return lax.dot_general(a, b, (((1,), (1,)), ((), ())), preferred_element_type=f32)


def dot_tn(a, b):
    return lax.dot_general(a, b, (((0,), (0,)), ((), ())), preferred_element_type=f32)


LOAD, STORE = "load", "store"


class Loaded:
    def __init__(self, source, target, sem):
        self.copy, self.target, self.here = pltpu.make_async_copy(source, target, sem), target, False
        self.copy.start()

    def get(self):
        if not self.here:
            self.copy.wait()
            self.here = True
        return self.target


class Stored:
    def __init__(self, target, source, sem):
        self.target, self.ref, self.sem, self.sent = target, source, sem, []

    def send(self, index=None):
        source, target = self.ref, self.target
        if index is not None:
            source, target = source.at[index], target.at[index]
        self.sent.append(pltpu.make_async_copy(source, target, self.sem))
        self.sent[-1].start()

    def finish(self):
        for copy in self.sent:
            copy.wait()


def call(kernel, ins, outs, scratch, operands, after=(), aliases=None, limit=62, cost=10**11):
    n_in, skip, n_out, n_scratch = len(operands), len(after), len(outs), len(scratch)
    scratch = list(scratch)
    for x, spec in [*zip(operands, ins), *outs]:
        if spec in (LOAD, STORE):
            scratch += [pltpu.VMEM(x.shape, x.dtype), pltpu.SemaphoreType.DMA]

    def run(*refs):
        given, results = list(refs[:n_in]), list(refs[n_in + skip : n_in + skip + n_out])
        rest = refs[n_in + skip + n_out :]
        own, extra = rest[:n_scratch], list(rest[n_scratch:])
        for k, spec in enumerate(ins):
            if spec == LOAD:
                given[k] = Loaded(given[k], extra.pop(0), extra.pop(0))
        for k, (_, spec) in enumerate(outs):
            if spec == STORE:
                results[k] = Stored(results[k], extra.pop(0), extra.pop(0))
        kernel(*given, *results, *own)
        for k, (_, spec) in enumerate(outs):
            if spec == STORE:
                results[k].finish()

    base = kernel.func if isinstance(kernel, functools.partial) else kernel
    suffix = str(kernel.args[0]) if isinstance(kernel, functools.partial) else ""
    name = base.__name__.strip("<>").replace("_kernel", "") + suffix

    def place(spec):
        return ANY if spec in (LOAD, STORE) else spec

    return pl.pallas_call(
        run,
        name=name,
        in_specs=[place(spec) for spec in ins] + [ANY] * skip,
        out_specs=[place(o[1]) for o in outs],
        out_shape=[o[0] for o in outs],
        scratch_shapes=scratch,
        input_output_aliases=aliases or {},
        compiler_params=pltpu.CompilerParams(vmem_limit_bytes=limit * MIB),
        cost_estimate=pl.CostEstimate(flops=cost, bytes_accessed=1000, transcendentals=0),
    )(*operands, *after)


def shape(*dims, dtype=bf16):
    return jax.ShapeDtypeStruct(dims, dtype)


def load_pieces(place, pieces, target, first, rows, sem):
    for j in range(8):
        for i in range(4):
            at = place[2 * (4 * j + i)]
            lane = pl.multiple_of(place[2 * (4 * j + i) + 1] * 128, 128)
            pltpu.make_async_copy(
                pieces[j].at[i, pl.ds(first, rows), :],
                target.at[at, :, pl.ds(lane, 128)],
                sem,
            ).start()


def fill(info, blocks, target):
    for k in range(4):
        at = pl.multiple_of((info[1] ^ k) * BLOCK, BLOCK)
        target[pl.ds(at, BLOCK), :] = blocks[k][...]


def wait_all(target, sem):
    pltpu.make_async_copy(target, target, sem).wait()


def fetch(info, blocks, target, sem):
    for k in range(4):
        at = pl.multiple_of((info[1] ^ k) * BLOCK, BLOCK)
        pltpu.make_async_copy(blocks[k], target.at[pl.ds(at, BLOCK), :], sem).start()


def qkv_kernel(info, *refs):
    acts, pieces = refs[:4], refs[4:12]
    cosine, sine, keep, away, weight, act, sems = *refs[12:15], refs[15:18], *refs[18:]
    core = info[0]
    fetch(info, acts, act, sems.at[0])
    load_pieces(info.at[pl.ds(8, 64)], pieces, weight, 0, 768, sems.at[1])
    wait_all(act, sems.at[0])
    wait_all(weight, sems.at[1])
    cosine, sine = cosine.get(), sine.get()
    for which, out in ((1, away), (0, keep)):
        s = core ^ which
        for m in range(3):
            got = dot_nt(act[...], weight[s, pl.ds(WIDTH * m, WIDTH), :])
            place = out.ref.at[m] if which == 0 else out[m].ref
            if m == 2:
                place[...] = got.astype(bf16)
            for h in range(2 if m < 2 else 0):
                v = got[:, HEAD_DIM * h : HEAD_DIM * h + HEAD_DIM]
                turned = pltpu.roll(v, HEAD_DIM // 2, 1)
                place[:, HEAD_DIM * h : HEAD_DIM * h + HEAD_DIM] = (
                    v * cosine[...] + turned * sine[...]
                ).astype(bf16)
            if which == 0:
                out.send(m)
            else:
                out[m].send()


def project_qkv(info, acts, pieces, cosine, sine, after=()):
    return call(
        qkv_kernel,
        [SMEM] + [ANY] * 12 + [LOAD] * 2,
        [(shape(3, 512, WIDTH), STORE)] + [(shape(512, WIDTH), STORE)] * 3,
        [pltpu.VMEM((2, 768, D), bf16), ROWS, pltpu.SemaphoreType.DMA((2,))],
        [info, *acts, *pieces, cosine, sine],
        cost=1000,
        after=after,
    )


TILE = 256


def masked_scores(q, k, seg_col, seg_row, first, count):
    s = dot_nt(q, k) * HEAD_DIM**-0.5
    rows = first + lax.broadcasted_iota(jnp.int32, (TILE, count), 0)
    cols = lax.broadcasted_iota(jnp.int32, (TILE, count), 1)
    ok = (cols <= rows) & (seg_col == seg_row)
    return jnp.where(ok, s, -1e30)


def softmax(s):
    e = jnp.exp(s - jnp.max(s, axis=-1, keepdims=True))
    return e * (1.0 / jnp.sum(e, axis=-1, keepdims=True))


def to_order(info, mine, got, target, m):
    for h, source in ((0, mine.at[m]), (1, got)):
        at = pl.multiple_of((info[0] ^ h) * 512, 512)
        target[m, pl.ds(at, 512), :] = source[...]


def from_order(info, source, m, target, h):
    at = pl.multiple_of((info[0] ^ h) * 512, 512)
    target[m] = source[m, pl.ds(at, 512), :]


def attend_kernel(info, mine, *refs):
    got, (seg_col, seg_row, keep, away, qkv, result) = refs[:3], refs[3:]
    for m in range(3):
        to_order(info, mine, got[m], qkv, m)
    for h in range(2):
        lanes = slice(HEAD_DIM * h, HEAD_DIM * h + HEAD_DIM)
        for t in range(1024 // TILE):
            n = TILE * (t + 1)
            rows = slice(TILE * t, n)
            s = masked_scores(
                qkv[0, rows, lanes], qkv[1, :n, lanes], seg_col[rows, :], seg_row[:, :n],
                TILE * t, n,
            )
            result[0, rows, lanes] = dot_nn(softmax(s).astype(bf16), qkv[2, :n, lanes]).astype(bf16)
    from_order(info, result, 0, away, 1)
    from_order(info, result, 0, keep, 0)


def attend(info, mine, got, seg_col, seg_row, after=()):
    return call(
        attend_kernel,
        [SMEM] + [VMEM] * 6,
        [(shape(1, 512, WIDTH), VMEM)] * 2,
        [pltpu.VMEM((3, 1024, WIDTH), bf16), pltpu.VMEM((1, 1024, WIDTH), bf16)],
        [info, mine, *got, seg_col, seg_row],
        limit=20,
        cost=1000,
        after=after,
    )


def attend_back_kernel(info, mine, *refs):
    got, (g_mine, g_got, seg_col, seg_row, cosine, sine, keep, away) = refs[:3], refs[3:11]
    qkv, grad, total, result = refs[11:]
    scale = HEAD_DIM**-0.5
    for m in range(3):
        to_order(info, mine, got[m], qkv, m)
    to_order(info, g_mine, g_got.at[0], grad, 0)
    for h in range(2):
        lanes = slice(HEAD_DIM * h, HEAD_DIM * h + HEAD_DIM)
        total[...] = jnp.zeros_like(total)
        for t in range(1024 // TILE):
            n = TILE * (t + 1)
            rows = slice(TILE * t, n)
            q, g = qkv[0, rows, lanes], grad[0, rows, lanes]
            s = masked_scores(q, qkv[1, :n, lanes], seg_col[rows, :], seg_row[:, :n], TILE * t, n)
            p = softmax(s)
            dp = dot_nt(g, qkv[2, :n, lanes])
            ds = (p * (dp - jnp.sum(p * dp, axis=-1, keepdims=True))).astype(bf16)
            total[0, rows, :] = dot_nn(ds, qkv[1, :n, lanes]) * scale
            total[1, :n, :] += dot_tn(ds, q) * scale
            total[2, :n, :] += dot_tn(p.astype(bf16), g)
        for m in range(2):
            v = total[m]
            turned = pltpu.roll(v, HEAD_DIM // 2, 1)
            result[m, :, lanes] = (v * cosine[...] - turned * sine[...]).astype(bf16)
        result[2, :, lanes] = total[2].astype(bf16)
    for m in range(3):
        from_order(info, result, m, away, 1)
        from_order(info, result, m, keep, 0)


def attend_back(info, mine, got, g_mine, g_got, seg_col, seg_row, cosine, sine, after=()):
    return call(
        attend_back_kernel,
        [SMEM] + [VMEM] * 10,
        [(shape(3, 512, WIDTH), VMEM)] * 2,
        [
            pltpu.VMEM((3, 1024, WIDTH), bf16),
            pltpu.VMEM((1, 1024, WIDTH), bf16),
            pltpu.VMEM((3, 1024, HEAD_DIM), f32),
            pltpu.VMEM((3, 1024, WIDTH), bf16),
        ],
        [info, mine, *got, g_mine, g_got, seg_col, seg_row, cosine, sine],
        cost=1000,
        after=after,
    )


def write_blocks(info, total, outs):
    for k in range(4):
        at = pl.multiple_of((info[1] ^ k) * BLOCK, BLOCK)
        outs[k][...] = total[pl.ds(at, BLOCK), :].astype(outs[k].dtype)


BLOCK_OUTS = [(shape(BLOCK, D, dtype=f32), VMEM)] + [(shape(BLOCK, D), VMEM)] * 3


def out_kernel(info, mine, got, *refs):
    pieces, outs, (weight, total, sem) = refs[:8], refs[8:12], refs[12:]
    core = info[0]
    load_pieces(info.at[pl.ds(8, 64)], pieces, weight, 768, 256, sem)
    mine, got = mine.get(), got.get()
    wait_all(weight, sem)
    total[...] = dot_nn(mine[0], weight[core]) + dot_nn(got[0], weight[core ^ 1])
    write_blocks(info, total, outs)


def project_out(info, mine, got, pieces, after=()):
    return call(
        out_kernel,
        [SMEM] + [LOAD] * 2 + [ANY] * 8,
        BLOCK_OUTS,
        [pltpu.VMEM((2, 256, D), bf16), TOTAL, pltpu.SemaphoreType.DMA],
        [info, mine, got, *pieces],
        limit=20,
        cost=1000,
        after=after,
    )


def out_back_kernel(info, *refs):
    acts, pieces = refs[:4], refs[4:12]
    keep, away, weight, act, sems = refs[12:]
    core = info[0]
    fetch(info, acts, act, sems.at[0])
    load_pieces(info.at[pl.ds(8, 64)], pieces, weight, 768, 256, sems.at[1])
    wait_all(act, sems.at[0])
    wait_all(weight, sems.at[1])
    for which, out in ((1, away), (0, keep)):
        out.ref[0] = dot_nt(act[...], weight[core ^ which]).astype(bf16)
        out.send()


def project_out_back(info, acts, pieces, after=()):
    return call(
        out_back_kernel,
        [SMEM] + [ANY] * 12,
        [(shape(1, 512, WIDTH), STORE)] * 2,
        [pltpu.VMEM((2, 256, D), bf16), ROWS, pltpu.SemaphoreType.DMA((2,))],
        [info, *acts, *pieces],
        after=after,
    )


def qkv_back_kernel(info, mine, got, *refs):
    pieces, acts = refs[:8], refs[8:12]
    out, gain, weight, total, act, sem, act_sem = refs[12:]
    fetch(info, acts, act, act_sem)
    core = info[0]
    load_pieces(info.at[pl.ds(8, 64)], pieces, weight, 0, 768, sem)
    wait_all(weight, sem)
    mine, got = mine.get(), got.get()
    total[...] = dot_nn(jnp.concatenate([mine[m] for m in range(3)], axis=1), weight[core])
    total[...] += dot_nn(jnp.concatenate([got[m] for m in range(3)], axis=1), weight[core ^ 1])
    out.ref[...] = total[...].astype(bf16)
    out.send()
    wait_all(act, act_sem)
    gain[...] = jnp.sum(total[...] * act[...].astype(f32), axis=0, keepdims=True)


def project_qkv_back(info, mine, got, pieces, acts, after=()):
    return call(
        qkv_back_kernel,
        [SMEM] + [LOAD] * 2 + [ANY] * 12,
        [(shape(512, D), STORE), (shape(1, D, dtype=f32), VMEM)],
        [pltpu.VMEM((2, 768, D), bf16), TOTAL, ROWS]
        + [pltpu.SemaphoreType.DMA] * 2,
        [info, mine, got, *pieces, *acts],
        after=after,
    )


def load_gathered(weights, target, s, first, rows, row, sem):
    for x in range(4):
        for y in range(2):
            for c in range(2):
                f = x * 4 + y * 2 + c
                pltpu.make_async_copy(
                    weights.at[x * 8 + y * 4 + s * 2 + c, pl.ds(first, rows), :],
                    target.at[s, pl.ds(row, rows), f * 128 : f * 128 + 128],
                    sem,
                ).start()


def mlp_kernel(info, *refs):
    acts, cots, weights = refs[:4], refs[4:8], refs[8]
    hid, gate_grad, up_grad = refs[9:12]
    outs = refs[12:16]
    weight, act, cot, total, sems = refs[16:]
    n = UNITS
    fetch(info, acts, act, sems.at[3])
    load_gathered(weights, weight, 0, 0, n, 0, sems.at[0])
    load_gathered(weights, weight, 0, n, 2 * n, n, sems.at[1])
    fetch(info, cots, cot, sems.at[4])
    wait_all(act, sems.at[3])
    for s in range(2):
        if s == 0:
            wait_all(weight.at[0, pl.ds(0, n), :], sems.at[0])
        else:
            wait_all(weight.at[1], sems.at[2])
        gate = dot_nt(act[...], weight[s, pl.ds(0, n), :])
        if s == 0:
            load_gathered(weights, weight, 1, 0, 3 * n, 0, sems.at[2])
            wait_all(weight.at[0, pl.ds(n, 2 * n), :], sems.at[1])
            wait_all(cot, sems.at[4])
        up = dot_nt(act[...], weight[s, pl.ds(n, n), :])
        hg = dot_nt(cot[...], weight[s, pl.ds(2 * n, n), :])
        sig = 1.0 / (1.0 + jnp.exp(-gate))
        silu = gate * sig
        hid.ref[s] = (silu * up).astype(bf16)
        gate_grad.ref[s] = (hg * up * (sig * (1.0 + gate * (1.0 - sig)))).astype(bf16)
        up_grad.ref[s] = (hg * silu).astype(bf16)
        for result in (hid, gate_grad, up_grad):
            result.send(s)
        part = dot_nn(gate_grad.ref[s], weight[s, pl.ds(0, n), :]) + dot_nn(
            up_grad.ref[s], weight[s, pl.ds(n, n), :]
        )
        if s == 0:
            total[...] = part
        else:
            total[...] += part
    for k in (2, 1, 3, 0):
        at = pl.multiple_of((info[1] ^ k) * BLOCK, BLOCK)
        outs[k].ref[...] = total[pl.ds(at, BLOCK), :].astype(outs[k].ref.dtype)
        outs[k].send()


def mlp(info, acts, cots, weights, after=()):
    return call(
        mlp_kernel,
        [SMEM] + [ANY] * 9,
        [(shape(2, 512, UNITS), STORE)] * 3
        + [(shape(BLOCK, D, dtype=f32), STORE)]
        + [(shape(BLOCK, D), STORE)] * 3,
        [pltpu.VMEM((2, 3 * UNITS, D), bf16), ROWS, ROWS, TOTAL, pltpu.SemaphoreType.DMA((5,))],
        [info, *acts, *cots, weights],
        after=after,
    )


def down_kernel(hid, weights, out, weight, total, sems):
    for s in range(2):
        load_gathered(weights, weight, s, 2 * UNITS, UNITS, 0, sems.at[s])
    hid = hid.get()
    wait_all(weight.at[0], sems.at[0])
    total[...] = dot_nn(hid[0], weight[0])
    wait_all(weight.at[1], sems.at[1])
    out.ref[...] = (total[...] + dot_nn(hid[1], weight[1])).astype(bf16)
    out.send()


def project_down(hid, weights, after=()):
    return call(
        down_kernel,
        [LOAD, ANY],
        [(shape(512, D), STORE)],
        [pltpu.VMEM((2, UNITS, D), bf16), TOTAL, pltpu.SemaphoreType.DMA((2,))],
        [hid, weights],
        after=after,
    )


def half_features(info, source, target, which):
    core, x, y = info[0], info[2], info[3]
    for dx in range(4):
        for dlo in range(2):
            lane = ((x ^ dx) * 4 + (y ^ dlo) * 2 + (core ^ which)) * 128
            b = 2 * dx + dlo
            target[:, 128 * b : 128 * b + 128] = source[:, pl.ds(pl.multiple_of(lane, 128), 128)]


class Joined:
    def __init__(self, ref):
        self.ref = ref

    def __getitem__(self, j):
        return self.ref.at[j]


def send_blocks(on_core, stage, slot, outs, rows, count, h, sem):
    def send(c):
        for dx in range(4):
            for dlo in range(2):
                dy = dlo + 2 * h
                i, j = (dx, dy) if c == 0 else (dy, dx)
                pltpu.make_async_copy(
                    stage.at[slot, 2 * dx + dlo, pl.ds(0, count), :],
                    outs[j].at[i, rows, :],
                    sem,
                ).start()

    pl.when(on_core == 0)(functools.partial(send, 0))
    pl.when(on_core == 1)(functools.partial(send, 1))


def half_grads(on_core, lefts, rights, spans, outs, stage, sems, got=None):
    step = 0
    for m, (first, count) in enumerate(spans):
        right = rights[m]()
        rows = pl.ds(first, count)
        for h in range(2):
            slot = step % 2
            part = dot_tn(lefts(h, m), right[...])
            if step >= 2:
                before = pl.ds(0, spans[(step - 2) // 2][1])
                wait_all(stage.at[slot, :, before, :], sems.at[slot])
            more = got(m) if got else None
            for dx in range(4):
                for dlo in range(2):
                    b, dy = 2 * dx + dlo, dlo + 2 * h
                    block = part[:, 128 * b : 128 * b + 128]
                    if got:
                        i = jnp.where(on_core == 0, dx, dy)
                        j = jnp.where(on_core == 0, dy, dx)
                        block = block + more[j, i, rows, :].astype(f32)
                    stage[slot, b, 0:count, :] = block.astype(bf16)
            send_blocks(on_core, stage, slot, outs, rows, count, h, sems.at[slot])
            step += 1
    for slot in range(2):
        wait_all(stage.at[slot, :, pl.ds(0, spans[-1][1]), :], sems.at[slot])


def load_got(pieces, target, spans, sems):
    for m, (first, count) in enumerate(spans):
        rows = pl.ds(first, count)
        for j in range(4):
            pltpu.make_async_copy(
                pieces[j].at[:, rows, :], target.at[j, :, rows, :], sems.at[m]
            ).start()
    waited = []

    def got(m):
        if m not in waited:
            waited.append(m)
            part = target.at[:, :, pl.ds(*spans[m]), :]
            pltpu.make_async_copy(part, part, sems.at[m]).wait()
        return target

    return got


MLP_SPANS = [(0, UNITS), (UNITS, UNITS), (2 * UNITS, UNITS)]
ATTN_SPANS = [(0, 3 * WIDTH), (3 * WIDTH, WIDTH)]


def mlp_rights(info, acts, cots, act, cot, act_half, cot_half, sems, which):
    fetch(info, acts, act, sems.at[0])
    fetch(info, cots, cot, sems.at[1])

    def first():
        wait_all(act, sems.at[0])
        half_features(info, act, act_half, which)
        return act_half

    def last():
        wait_all(cot, sems.at[1])
        half_features(info, cot, cot_half, which)
        return cot_half

    return first, lambda: act_half, last


def mlp_grads_kernel(which, info, gate_grad, up_grad, hid, *refs):
    acts, cots, refs = refs[:4], refs[4:8], refs[8:]
    got = None
    if which == 0:
        piece, outs, refs = Joined(refs[0]), refs[2:6], refs[7:]
    else:
        outs, refs = Joined(refs[0]), refs[1:]
    act, cot, act_half, cot_half, stage, sems, in_sems = refs[:7]
    rights = mlp_rights(info, acts, cots, act, cot, act_half, cot_half, in_sems, which)
    if which == 0:
        got = load_got(piece, refs[7], MLP_SPANS, refs[8])
    sources = (gate_grad, up_grad, hid)
    half_grads(
        info[0] ^ which, lambda h, m: sources[m].get()[info[4] ^ h], rights, MLP_SPANS, outs,
        stage, sems, got,
    )


def mlp_grads(which, info, hid, gate_grad, up_grad, acts, cots, got=(), passed=(), after=()):
    scratch = [
        ROWS, ROWS, HALF, HALF, pltpu.VMEM((2, 8, UNITS, 128), bf16),
        pltpu.SemaphoreType.DMA((2,)), pltpu.SemaphoreType.DMA((2,)),
    ]
    if which == 0:
        scratch += [pltpu.VMEM((4, 4, 3 * UNITS, 128), bf16), pltpu.SemaphoreType.DMA((3,))]
    return call(
        functools.partial(mlp_grads_kernel, which),
        [SMEM] + [LOAD] * 3 + [ANY] * (8 + len(got) + len(passed)),
        [(shape(4, 3 * UNITS, 128), ANY)] * 4 + [(shape(*v.shape), ANY) for v in passed]
        if which == 0 else [(shape(4, 4, 3 * UNITS, 128), ANY)],
        scratch,
        [info, gate_grad, up_grad, hid, *acts, *cots, *got, *passed],
        after=after,
        aliases={13: 4} if passed else None,
    )


def split_gains(gains, total, halves):
    for b in range(16):
        lanes = slice(128 * b, 128 * b + 128)
        total[b : b + 1, :] = gains[0:1, lanes]
        total[16 + b : 17 + b, :] = gains[1:2, lanes]
    coarse = total[...].astype(bf16)
    halves[0:32, :] = coarse
    halves[32:64, :] = (total[...] - coarse.astype(f32)).astype(bf16)


def attn_grads_kernel(which, info, mine, got_heads, att_mine, att_got, *refs):
    mids, acts, refs = refs[:4], refs[4:8], refs[8:]
    got = None
    if which == 0:
        piece, gains, outs, refs = Joined(refs[0]), refs[1], refs[2:6], refs[6:]
        split_gains(gains, *refs[10:12])
        for j in range(4):
            for i in range(4):
                pltpu.make_async_copy(
                    refs[11].at[pl.ds(16 * i, 16), :],
                    outs[j].at[i, pl.ds(4 * WIDTH, 16), :],
                    refs[12],
                ).start()
    else:
        outs, refs = Joined(refs[0]), refs[1:]
    left, act_half, mid_half, stage, sems, act, mid, in_sems = refs[:8]
    fetch(info, acts, act, in_sems.at[0])
    fetch(info, mids, mid, in_sems.at[1])
    if which == 0:
        got = load_got(piece, refs[8], ATTN_SPANS, refs[9])
    for w, (grads, att) in enumerate(((mine, att_mine), (got_heads, att_got))):
        for m in range(3):
            left[w, :, WIDTH * m : WIDTH * m + WIDTH] = grads.get()[m]
        left[w, :, 3 * WIDTH :] = att.get()[0]

    def first():
        wait_all(act, in_sems.at[0])
        half_features(info, act, act_half, which)
        return act_half

    def last():
        wait_all(mid, in_sems.at[1])
        half_features(info, mid, mid_half, which)
        return mid_half

    half_grads(
        info[0] ^ which,
        lambda h, m: left[
            info[0] ^ info[4] ^ h, :, ATTN_SPANS[m][0] : sum(ATTN_SPANS[m])
        ],
        (first, last), ATTN_SPANS, outs, stage, sems, got,
    )
    if which == 0:
        for j in range(4):
            wait_all(refs[11], refs[12])


def attn_grads(which, info, operands, got=(), gains=(), after=()):
    scratch = [
        pltpu.VMEM((2, 512, 4 * WIDTH), bf16), HALF, HALF,
        pltpu.VMEM((2, 8, 3 * WIDTH, 128), bf16), pltpu.SemaphoreType.DMA((2,)),
        ROWS, ROWS, pltpu.SemaphoreType.DMA((2,)),
    ]
    if which == 0:
        scratch += [
            pltpu.VMEM((4, 4, 4 * WIDTH, 128), bf16), pltpu.SemaphoreType.DMA((2,)),
            pltpu.VMEM((32, 128), f32), pltpu.VMEM((64, 128), bf16), pltpu.SemaphoreType.DMA,
        ]
    return call(
        functools.partial(attn_grads_kernel, which),
        [SMEM] + [LOAD] * 4 + [ANY] * (8 + len(got)) + [VMEM] * len(gains),
        [(shape(4, 4 * WIDTH + 16, 128), ANY)] * 4 if which == 0 else
        [(shape(4, 4, 4 * WIDTH, 128), ANY)],
        scratch,
        [info, *operands, *got, *gains],
        after=after,
    )


def norm_back(x, gain, gradient):
    inverse = lax.rsqrt(jnp.mean(x * x, axis=-1, keepdims=True) + epsilon)
    scaled = gradient * gain
    mean_term = jnp.mean(scaled * x, axis=-1, keepdims=True)
    back = inverse * scaled - x * (inverse * inverse * inverse) * mean_term
    return back, inverse


def middle_back_kernel(middle, gain, cotangent, *refs):
    gradient, (out, low, gain_part) = refs[:4], refs[4:]
    x, e = middle[...], gradient[0][...]
    for v in gradient[1:]:
        e = e + v[...].astype(f32)
    back, inverse = norm_back(x, gain[...], e)
    total = cotangent[...].astype(f32) + back
    out[...] = total
    low[...] = total.astype(bf16)
    gain_part[...] = jnp.sum(e * x * inverse, axis=0, keepdims=True)


def middle_back(middle, gain, gradient, cotangent, after):
    return call(
        middle_back_kernel,
        [VMEM] * 7,
        [
            (shape(BLOCK, D, dtype=f32), VMEM),
            (shape(BLOCK, D), VMEM),
            (shape(1, D, dtype=f32), VMEM),
        ],
        [],
        [middle, gain[None], cotangent, *gradient],
        after=after,
    )


def input_back_kernel(stream, gain, gradient, middle, out):
    back, _ = norm_back(stream[0:BLOCK, :].astype(f32), gain[...], gradient[...].astype(f32))
    out[...] = (middle[...] + back).astype(bf16)


def input_back(stream, gain, gradient, middle, after):
    return call(
        input_back_kernel,
        [VMEM] * 4,
        [(shape(BLOCK, D), VMEM)],
        [],
        [stream, gain[None], gradient, middle],
        after=after,
    )[0]


def second_sum(parts, gains=False, after=(), passed=()):
    rows = parts[0].shape[1] - 16 * gains
    more = 64 * gains

    def second_sum_kernel(*refs):
        sources, outs = refs[:4], refs[4 + len(passed) : 8 + len(passed)]
        ins, sems = refs[-2:]
        for k in (1, 2, 3, 0):
            for v in range(4):
                pltpu.make_async_copy(sources[v].at[k], ins.at[k, v], sems.at[k]).start()
        if gains:
            for k in range(4):
                wait_all(ins.at[k], sems.at[k])
            low = pl.ds(rows, 16)
            part = []
            for v in range(4):
                coarse = jnp.concatenate([ins[0, v, low, :], ins[1, v, low, :]], axis=0)
                fine = jnp.concatenate([ins[2, v, low, :], ins[3, v, low, :]], axis=0)
                part.append(coarse.astype(f32) + fine.astype(f32))
            total = (part[0] + part[1]) + (part[2] + part[3])
            coarse = total.astype(bf16)
            fine = (total - coarse.astype(f32)).astype(bf16)
        for k in (1, 2, 3, 0):
            out = outs[k].ref
            if not gains:
                wait_all(ins.at[k], sems.at[k])
            total = ins[k, 0, 0:rows, :].astype(f32)
            for v in range(1, 4):
                total = total + ins[k, v, 0:rows, :].astype(f32)
            out[0:rows, :] = total.astype(out.dtype)
            if gains:
                out[rows : rows + 32, :] = coarse.astype(out.dtype)
                out[rows + 32 :, :] = fine.astype(out.dtype)
            outs[k].send()

    return call(
        second_sum_kernel,
        [ANY] * (4 + len(passed)),
        [(shape(rows + more, 128, dtype=f32 if k == 0 else bf16), STORE) for k in range(4)]
        + [(shape(*v.shape), ANY) for v in passed],
        [pltpu.VMEM((4, 4, *parts[0].shape[1:]), bf16), pltpu.SemaphoreType.DMA((4,))],
        [*parts, *passed],
        after=after,
        aliases={4: 4} if passed else None,
    )


def final_sum(parts, plan, after=()):
    def final_sum_kernel(*refs):
        ins, outs = refs[:4], refs[4:]
        for (first, rows, turn), out in zip(plan, outs):
            part = [v[first : first + rows, :].astype(f32) for v in ins]
            total = (part[0] + part[1]) + (part[2] + part[3])
            out[...] = total.T if turn else total

    outs = [
        (shape(*((128, rows) if turn else (rows, 128)), dtype=f32), VMEM)
        for _, rows, turn in plan
    ]
    return call(final_sum_kernel, [VMEM] * 4, outs, [], list(parts), limit=24, cost=1000, after=after)


def widen_kernel(value, out):
    out[...] = value[...].astype(f32)


def widen(value, after=()):
    return call(
        widen_kernel,
        [VMEM],
        [(shape(*value.shape, dtype=f32), VMEM)],
        [],
        [value],
        after=after,
        cost=1000,
    )[0]


def stack_attn_kernel(query, key, value, output, out):
    w = WIDTH
    for m, ref in enumerate((query, key, value)):
        out[w * m : w * m + w, :] = ref[...].T
    out[3 * w :, :] = output[...]


def stack_attn(query, key, value, output):
    return call(
        stack_attn_kernel,
        [VMEM] * 4,
        [(shape(4 * WIDTH, 128), VMEM)],
        [],
        [query, key, value, output],
        cost=1000,
    )[0]


def joined_kernel(stream, more, out):
    out[...] = (stream[...] + more[...].astype(f32)).astype(bf16)


def joined(stream, more, after):
    return call(
        joined_kernel,
        [VMEM] * 2,
        [(shape(BLOCK, D), VMEM)],
        [],
        [stream, more],
        after=after,
        cost=1000,
    )[0]


def stack_kernel(*refs):
    gate, up, down, out = refs[0], refs[1], refs[2], refs[-1]
    out[0:UNITS, :] = gate[...]
    out[UNITS : 2 * UNITS, :] = up[...]
    out[2 * UNITS :, :] = down[...]


def stack_mlp(gate, up, down, after=()):
    return call(
        stack_kernel,
        [VMEM] * 3,
        [(shape(3 * UNITS, 128), VMEM)],
        [],
        [gate, up, down],
        after=after,
    )[0]


def copy_kernel(value, out):
    out[...] = value[...]


def copied(value, after):
    return call(copy_kernel, [VMEM], [(shape(*value.shape, dtype=value.dtype), VMEM)], [], [value], after=after)[0]


def held_kernel(*refs):
    del refs


def held_all(values, after):
    return call(
        held_kernel,
        [ANY] * len(values),
        [(shape(*v.shape, dtype=v.dtype), ANY) for v in values],
        [],
        values,
        after=after,
        aliases={k: k for k in range(len(values))},
        cost=1000,
    )


def held(value, after):
    return held_all([value], after)[0]


def row_kernel(*refs):
    parts, row, twin = refs[:4], refs[4], refs[5]
    copies = []
    for k in range(4):
        row.ref[k] = parts[k].get()[...]
        row.send(k)
        copies.append(pltpu.make_async_copy(row.ref.at[k], twin.at[k], refs[6].at[k]))
        copies[-1].start()
    for copy in copies:
        copy.wait()


def joined_row(parts):
    out = shape(4, *parts[0].shape)
    return call(
        row_kernel,
        [LOAD] * 4,
        [(out, STORE), (out, ANY)],
        [pltpu.SemaphoreType.DMA((4,))],
        parts,
        cost=1000,
    )


def norm_kernel(stream, gain, out):
    x = stream[0:BLOCK, :].astype(f32)
    inverse = lax.rsqrt(jnp.mean(x * x, axis=-1, keepdims=True) + epsilon)
    out[...] = (x * inverse * gain[...]).astype(bf16)


def normed(stream, gain, after):
    return call(
        norm_kernel,
        [VMEM] * 2,
        [(shape(BLOCK, D), VMEM)],
        [],
        [stream, gain[None]],
        after=after,
    )[0]


def swap_bits(value, axes, change, name):
    sizes = [SIZES[a] for a in axes]
    pairs = []
    for index in np.ndindex(*sizes):
        pairs.append(
            (
                int(np.ravel_multi_index(index, sizes)),
                int(np.ravel_multi_index(change(*index), sizes)),
            )
        )
    with jax.named_scope(name):
        return lax.ppermute(value, axes if len(axes) > 1 else axes[0], pairs)


def over_z(value, k):
    return swap_bits(value, ("z",), lambda z: (z ^ k,), f"over_z{k}")


def over_x(value, k):
    return swap_bits(value, ("x",), lambda x: (x ^ k,), f"over_x{k}")


def over_y(value, k):
    return swap_bits(value, ("ylo", "yhi"), lambda lo, hi: (lo ^ (k & 1), hi ^ (k >> 1)), f"over_y{k}")


def over_core(value):
    return swap_bits(value, ("core",), lambda c: (c ^ 1,), "over_core")


def exchange(value):
    return swap_bits(value, ("core", "yhi"), lambda c, h: (h, c), "exchange")


def across(value, k, first):
    def change(x, lo, core, hi):
        if (core == 0) == first:
            return (x ^ k, lo, core, hi)
        return (x, lo ^ (k & 1), core, hi ^ (k >> 1))

    return swap_bits(value, ("x", "ylo", "core", "yhi"), change, f"across{k}" if first else f"second{k}")


def second_step(parts):
    return [parts[0]] + [across(parts[k], k, False) for k in (1, 2, 3)]


def first_step(parts):
    out = parts[0]
    for k in (1, 2, 3):
        out = out + across(parts[k], k, True).astype(f32)
    return out


def gather_tokens(value):
    return [value] + [over_z(value, k) for k in (1, 2, 3)]


def scatter_tokens(blocks):
    out = blocks[0]
    for k in (1, 2, 3):
        out = out + over_z(blocks[k], k).astype(f32)
    return out


def norm_forward(stream, gain):
    inverse = lax.rsqrt(jnp.mean(stream * stream, axis=-1, keepdims=True) + epsilon)
    return (stream * inverse * gain).astype(bf16), inverse


def body(
    block_input,
    segments,
    positions,
    attn_gain,
    w_query,
    w_key,
    w_value,
    w_output,
    mlp_gain,
    w_gate,
    w_up,
    w_down,
    cotangent,
):
    at_x, at_ylo, at_core, at_yhi, at_z = (lax.axis_index(a).astype(jnp.int32) for a in AXES)

    place = []
    for other in range(2):
        source = at_core ^ other
        for j in range(4):
            for i in range(4):
                dx = jnp.where(source == 0, i, j)
                dy = jnp.where(source == 0, j, i)
                place.append(at_yhi ^ (dy >> 1))
                place.append((at_x ^ dx) * 4 + (at_ylo ^ (dy & 1)) * 2 + source)
    zero = jnp.zeros((), jnp.int32)
    info = jnp.stack([at_core, at_z, at_x, at_ylo, at_yhi, zero, zero, zero] + place)

    extra = jnp.stack(
        [
            jnp.concatenate([positions // 64, positions % 64]),
            jnp.concatenate([segments, jnp.zeros_like(segments)]),
        ]
    ).astype(bf16)
    low_input = exchange(
        jnp.concatenate([block_input.astype(bf16), jnp.pad(extra, ((0, 14), (0, 0)))])
    )
    extra = low_input[BLOCK : BLOCK + 2].astype(f32)
    pos = extra[0, :1024] * 64.0 + extra[0, 1024:]
    segs = extra[1, :1024].astype(jnp.int32)
    seg_col, seg_row = segs[:, None], segs[None, :]
    frequency = base_freq ** (-(2.0 * jnp.arange(HEAD_DIM // 2, dtype=f32)) / HEAD_DIM)
    angles = pos[:, None] * frequency[None, :]
    cosine, sine = jnp.cos(angles), jnp.sin(angles)
    cosine = jnp.concatenate([cosine, cosine], axis=1)
    sine = jnp.concatenate([-sine, sine], axis=1)

    piece = stack_attn(w_query, w_key, w_value, w_output)
    grad_low = cotangent.astype(bf16)
    parts = [piece] + [across(piece, k, True) for k in (1, 2, 3)]
    row, twin = joined_row(parts)
    grad_low = held(grad_low, [row])
    act1 = normed(low_input, attn_gain, [row, grad_low])
    grad_low = exchange(grad_low)
    act1_all = gather_tokens(act1)
    pieces = [row, across(row, 1, False), None, across(row, 3, False)]
    pieces[2] = across(held(twin, [pieces[1], pieces[3], act1]), 2, False)
    pieces = pieces + [over_core(v) for v in pieces]
    cot_all = gather_tokens(grad_low)
    def own_rows(table):
        return lax.dynamic_slice_in_dim(table, at_core * 512, 512, axis=0)

    tables = [own_rows(cosine), own_rows(sine)]
    piece_mlp = stack_mlp(w_gate.T, w_up.T, w_down, after=[cosine, sine, seg_col, *tables])
    piece_mlp = held(piece_mlp, [*pieces[1:4], *act1_all[1:], grad_low])
    weights_mlp = lax.all_gather(piece_mlp, ("x", "ylo", "yhi", "core"))

    keep, *away = project_qkv(info, act1_all, pieces, *tables, after=[piece_mlp])
    qkv_mine, qkv_got = keep, [over_core(v) for v in away]
    keep, away = attend(info, qkv_mine, qkv_got, seg_col, seg_row, after=[cot_all[1], cot_all[3]])
    att_mine, att_got = keep, over_core(away)
    blocks = project_out(info, att_mine, att_got, pieces, after=cot_all[2:3])
    stream = low_input[:BLOCK].astype(f32)
    inverse1 = lax.rsqrt(jnp.mean(stream * stream, axis=-1, keepdims=True) + epsilon)
    middle = stream + scatter_tokens(blocks)
    act2, inverse2 = norm_forward(middle, mlp_gain)
    act2_all = gather_tokens(act2)

    hid, gate_grad, up_grad, *blocks = mlp(info, act2_all, cot_all, weights_mlp)
    grad_act2 = [blocks[0]] + [over_z(blocks[k], k) for k in (1, 2, 3)]
    operands = [info, hid, gate_grad, up_grad, act2_all, cot_all]
    (away,) = mlp_grads(1, *operands)
    got = over_core(away)
    (down,) = project_down(hid, weights_mlp, after=[away])
    grad_middle, middle_low, gain2_part = middle_back(
        middle, mlp_gain, grad_act2, grad_low, [down, got]
    )
    mid_all = gather_tokens(middle_low)
    *parts, down = mlp_grads(0, *operands, [got], [down], after=[middle_low])
    first, third = across(parts[1], 1, False), across(parts[3], 3, False)
    keep, away = project_out_back(info, mid_all, pieces, after=parts[:1])
    down = lax.psum_scatter(down, "z", tiled=True)
    keep, away = attend_back(
        info, qkv_mine, qkv_got, keep, over_core(away), seg_col, seg_row, cosine, sine
    )
    kept = held(parts[2], [keep, first, third])
    parts = [parts[0], first, across(kept, 2, False), third]
    g_mine, g_got = keep, over_core(away)
    operands = [g_mine, g_got, att_mine, att_got, *mid_all, *act1_all]
    (away,) = attn_grads(1, info, operands, after=[kept])
    got = over_core(away)
    partial, gain1_part = project_qkv_back(info, g_mine, g_got, pieces, act1_all, after=[away])
    parts = second_sum(parts, after=[gain1_part])
    out_block = exchange(joined(middle, down, parts[:1]))
    grad_act1 = lax.psum_scatter(partial, "z", tiled=True)
    parts = [parts[0]] + [across(parts[k], k, True) for k in (1, 2, 3)]
    gains = [jnp.concatenate([gain1_part / attn_gain, gain2_part])]
    outs = attn_grads(0, info, operands, [got], gains, after=parts[:1])
    grad_input = input_back(
        low_input, attn_gain, grad_act1, grad_middle, [outs[0]]
    )
    grad_gate, grad_up, grad_down = final_sum(
        parts, ((0, UNITS, False), (UNITS, UNITS, False), (2 * UNITS, UNITS, False)), [grad_input]
    )
    out_block = widen(out_block, [grad_input])
    *parts, grad_input = second_sum(
        second_step(outs), True, [grad_down, out_block], [grad_input]
    )
    grad_input = widen(exchange(grad_input))
    parts = [parts[0]] + [across(parts[k], k, True) for k in (1, 2, 3)]
    w, n = WIDTH, UNITS
    grad_query, grad_key, grad_value, grad_output, coarse, fine = final_sum(
        parts,
        ((0, w, True), (w, w, True), (2 * w, w, True), (3 * w, w, False),
         (4 * w, 32, False), (4 * w + 32, 32, False)),
        [grad_input],
    )
    gains = (coarse + fine).reshape(2, D)
    one, two, three = (over_z(gains, k) for k in (1, 2, 3))
    gains = (gains + one) + (two + three)
    gains = gains + over_core(gains)
    return (
        out_block,
        grad_input,
        gains[0],
        grad_query,
        grad_key,
        grad_value,
        grad_output,
        gains[1],
        grad_gate.T,
        grad_up.T,
        grad_down,
    )


def solution(mesh):
    inner = Mesh(np.asarray(mesh.devices).reshape([SIZES[a] for a in AXES]), AXES)
    dp, tensor = ("x", "ylo", "core"), ("yhi", "z")
    rows, wide, tall = P(dp + tensor, None), P(dp, tensor), P(tensor, dp)
    return jax.shard_map(
        body,
        mesh=inner,
        in_specs=(
            rows, P(dp), P(dp), P(), wide, wide, wide, tall, P(), wide, wide, tall, rows,
        ),
        out_specs=(rows, rows, P(), wide, wide, wide, tall, P(), wide, wide, tall),
        check_vma=False,
    )
```

```python
import functools

import jax
import jax.numpy as jnp
import numpy as np
from jax import lax
from jax.experimental import pallas as pl
from jax.experimental.pallas import tpu as pltpu
from jax.sharding import Mesh, PartitionSpec as P

HEAD_DIM = 128
BLOCK = 128
D = 2048
UNITS = 688
WIDTH = 256
epsilon = 1e-05
base_freq = 10000.0
AXES = ("x", "ylo", "core", "yhi", "z")
SIZES = {"x": 4, "ylo": 2, "core": 2, "yhi": 2, "z": 4}
bf16 = jnp.bfloat16
f32 = jnp.float32
MIB = 1 << 20
VMEM = pl.BlockSpec(memory_space=pltpu.VMEM)
SMEM = pl.BlockSpec(memory_space=pltpu.SMEM)
ANY = pl.BlockSpec(memory_space=pl.ANY)
TOTAL = pltpu.VMEM((512, D), f32)
ROWS = pltpu.VMEM((512, D), bf16)
HALF = pltpu.VMEM((512, D // 2), bf16)


def dot_nn(a, b):
    return lax.dot_general(a, b, (((1,), (0,)), ((), ())), preferred_element_type=f32)


def dot_nt(a, b):
    return lax.dot_general(a, b, (((1,), (1,)), ((), ())), preferred_element_type=f32)


def dot_tn(a, b):
    return lax.dot_general(a, b, (((0,), (0,)), ((), ())), preferred_element_type=f32)


LOAD, STORE = "load", "store"


class Loaded:
    def __init__(self, source, target, sem):
        self.copy, self.target, self.here = pltpu.make_async_copy(source, target, sem), target, False
        self.copy.start()

    def get(self):
        if not self.here:
            self.copy.wait()
            self.here = True
        return self.target


class Stored:
    def __init__(self, target, source, sem):
        self.target, self.ref, self.sem, self.sent = target, source, sem, []

    def send(self, index=None):
        source, target = self.ref, self.target
        if index is not None:
            source, target = source.at[index], target.at[index]
        self.sent.append(pltpu.make_async_copy(source, target, self.sem))
        self.sent[-1].start()

    def finish(self):
        for copy in self.sent:
            copy.wait()


def call(kernel, ins, outs, scratch, operands, after=(), aliases=None, limit=62, cost=10**11):
    n_in, skip, n_out, n_scratch = len(operands), len(after), len(outs), len(scratch)
    scratch = list(scratch)
    for x, spec in [*zip(operands, ins), *outs]:
        if spec in (LOAD, STORE):
            scratch += [pltpu.VMEM(x.shape, x.dtype), pltpu.SemaphoreType.DMA]

    def run(*refs):
        given, results = list(refs[:n_in]), list(refs[n_in + skip : n_in + skip + n_out])
        rest = refs[n_in + skip + n_out :]
        own, extra = rest[:n_scratch], list(rest[n_scratch:])
        for k, spec in enumerate(ins):
            if spec == LOAD:
                given[k] = Loaded(given[k], extra.pop(0), extra.pop(0))
        for k, (_, spec) in enumerate(outs):
            if spec == STORE:
                results[k] = Stored(results[k], extra.pop(0), extra.pop(0))
        kernel(*given, *results, *own)
        for k, (_, spec) in enumerate(outs):
            if spec == STORE:
                results[k].finish()

    base = kernel.func if isinstance(kernel, functools.partial) else kernel
    suffix = str(kernel.args[0]) if isinstance(kernel, functools.partial) else ""
    name = base.__name__.strip("<>").replace("_kernel", "") + suffix

    def place(spec):
        return ANY if spec in (LOAD, STORE) else spec

    return pl.pallas_call(
        run,
        name=name,
        in_specs=[place(spec) for spec in ins] + [ANY] * skip,
        out_specs=[place(o[1]) for o in outs],
        out_shape=[o[0] for o in outs],
        scratch_shapes=scratch,
        input_output_aliases=aliases or {},
        compiler_params=pltpu.CompilerParams(vmem_limit_bytes=limit * MIB),
        cost_estimate=pl.CostEstimate(flops=cost, bytes_accessed=1000, transcendentals=0),
    )(*operands, *after)


def shape(*dims, dtype=bf16):
    return jax.ShapeDtypeStruct(dims, dtype)


def load_pieces(place, pieces, target, first, rows, sem):
    for j in range(8):
        for i in range(4):
            at = place[2 * (4 * j + i)]
            lane = pl.multiple_of(place[2 * (4 * j + i) + 1] * 128, 128)
            pltpu.make_async_copy(
                pieces[j].at[i, pl.ds(first, rows), :],
                target.at[at, :, pl.ds(lane, 128)],
                sem,
            ).start()


def fill(info, blocks, target):
    for k in range(4):
        at = pl.multiple_of((info[1] ^ k) * BLOCK, BLOCK)
        target[pl.ds(at, BLOCK), :] = blocks[k][...]


def wait_all(target, sem):
    pltpu.make_async_copy(target, target, sem).wait()


def fetch(info, blocks, target, sem):
    for k in range(4):
        at = pl.multiple_of((info[1] ^ k) * BLOCK, BLOCK)
        pltpu.make_async_copy(blocks[k], target.at[pl.ds(at, BLOCK), :], sem).start()


def qkv_kernel(info, *refs):
    acts, pieces = refs[:4], refs[4:12]
    cosine, sine, keep, away, weight, act, sems = *refs[12:15], refs[15:18], *refs[18:]
    core = info[0]
    fetch(info, acts, act, sems.at[0])
    load_pieces(info.at[pl.ds(8, 64)], pieces, weight, 0, 768, sems.at[1])
    wait_all(act, sems.at[0])
    wait_all(weight, sems.at[1])
    cosine, sine = cosine.get(), sine.get()
    for which, out in ((1, away), (0, keep)):
        s = core ^ which
        for m in range(3):
            got = dot_nt(act[...], weight[s, pl.ds(WIDTH * m, WIDTH), :])
            place = out.ref.at[m] if which == 0 else out[m].ref
            if m == 2:
                place[...] = got.astype(bf16)
            for h in range(2 if m < 2 else 0):
                v = got[:, HEAD_DIM * h : HEAD_DIM * h + HEAD_DIM]
                turned = pltpu.roll(v, HEAD_DIM // 2, 1)
                place[:, HEAD_DIM * h : HEAD_DIM * h + HEAD_DIM] = (
                    v * cosine[...] + turned * sine[...]
                ).astype(bf16)
            if which == 0:
                out.send(m)
            else:
                out[m].send()


def project_qkv(info, acts, pieces, cosine, sine, after=()):
    return call(
        qkv_kernel,
        [SMEM] + [ANY] * 12 + [LOAD] * 2,
        [(shape(3, 512, WIDTH), STORE)] + [(shape(512, WIDTH), STORE)] * 3,
        [pltpu.VMEM((2, 768, D), bf16), ROWS, pltpu.SemaphoreType.DMA((2,))],
        [info, *acts, *pieces, cosine, sine],
        cost=1000,
        after=after,
    )


TILE = 256


def masked_scores(q, k, seg_col, seg_row, first, count):
    s = dot_nt(q, k) * HEAD_DIM**-0.5
    rows = first + lax.broadcasted_iota(jnp.int32, (TILE, count), 0)
    cols = lax.broadcasted_iota(jnp.int32, (TILE, count), 1)
    ok = (cols <= rows) & (seg_col == seg_row)
    return jnp.where(ok, s, -1e30)


def softmax(s):
    e = jnp.exp(s - jnp.max(s, axis=-1, keepdims=True))
    return e * (1.0 / jnp.sum(e, axis=-1, keepdims=True))


def to_order(info, mine, got, target, m):
    for h, source in ((0, mine.at[m]), (1, got)):
        at = pl.multiple_of((info[0] ^ h) * 512, 512)
        target[m, pl.ds(at, 512), :] = source[...]


def from_order(info, source, m, target, h):
    at = pl.multiple_of((info[0] ^ h) * 512, 512)
    target[m] = source[m, pl.ds(at, 512), :]


def attend_kernel(info, mine, *refs):
    got, (seg_col, seg_row, keep, away, qkv, result) = refs[:3], refs[3:]
    for m in range(3):
        to_order(info, mine, got[m], qkv, m)
    for h in range(2):
        lanes = slice(HEAD_DIM * h, HEAD_DIM * h + HEAD_DIM)
        for t in range(1024 // TILE):
            n = TILE * (t + 1)
            rows = slice(TILE * t, n)
            s = masked_scores(
                qkv[0, rows, lanes], qkv[1, :n, lanes], seg_col[rows, :], seg_row[:, :n],
                TILE * t, n,
            )
            result[0, rows, lanes] = dot_nn(softmax(s).astype(bf16), qkv[2, :n, lanes]).astype(bf16)
    from_order(info, result, 0, away, 1)
    from_order(info, result, 0, keep, 0)


def attend(info, mine, got, seg_col, seg_row, after=()):
    return call(
        attend_kernel,
        [SMEM] + [VMEM] * 6,
        [(shape(1, 512, WIDTH), VMEM)] * 2,
        [pltpu.VMEM((3, 1024, WIDTH), bf16), pltpu.VMEM((1, 1024, WIDTH), bf16)],
        [info, mine, *got, seg_col, seg_row],
        limit=20,
        cost=1000,
        after=after,
    )


def attend_back_kernel(info, mine, *refs):
    got, (g_mine, g_got, seg_col, seg_row, cosine, sine, keep, away) = refs[:3], refs[3:11]
    qkv, grad, total, result = refs[11:]
    scale = HEAD_DIM**-0.5
    for m in range(3):
        to_order(info, mine, got[m], qkv, m)
    to_order(info, g_mine, g_got.at[0], grad, 0)
    for h in range(2):
        lanes = slice(HEAD_DIM * h, HEAD_DIM * h + HEAD_DIM)
        total[...] = jnp.zeros_like(total)
        for t in range(1024 // TILE):
            n = TILE * (t + 1)
            rows = slice(TILE * t, n)
            q, g = qkv[0, rows, lanes], grad[0, rows, lanes]
            s = masked_scores(q, qkv[1, :n, lanes], seg_col[rows, :], seg_row[:, :n], TILE * t, n)
            p = softmax(s)
            dp = dot_nt(g, qkv[2, :n, lanes])
            ds = (p * (dp - jnp.sum(p * dp, axis=-1, keepdims=True))).astype(bf16)
            total[0, rows, :] = dot_nn(ds, qkv[1, :n, lanes]) * scale
            total[1, :n, :] += dot_tn(ds, q) * scale
            total[2, :n, :] += dot_tn(p.astype(bf16), g)
        for m in range(2):
            v = total[m]
            turned = pltpu.roll(v, HEAD_DIM // 2, 1)
            result[m, :, lanes] = (v * cosine[...] - turned * sine[...]).astype(bf16)
        result[2, :, lanes] = total[2].astype(bf16)
    for m in range(3):
        from_order(info, result, m, away, 1)
        from_order(info, result, m, keep, 0)


def attend_back(info, mine, got, g_mine, g_got, seg_col, seg_row, cosine, sine, after=()):
    return call(
        attend_back_kernel,
        [SMEM] + [VMEM] * 10,
        [(shape(3, 512, WIDTH), VMEM)] * 2,
        [
            pltpu.VMEM((3, 1024, WIDTH), bf16),
            pltpu.VMEM((1, 1024, WIDTH), bf16),
            pltpu.VMEM((3, 1024, HEAD_DIM), f32),
            pltpu.VMEM((3, 1024, WIDTH), bf16),
        ],
        [info, mine, *got, g_mine, g_got, seg_col, seg_row, cosine, sine],
        cost=1000,
        after=after,
    )


def write_blocks(info, total, outs):
    for k in range(4):
        at = pl.multiple_of((info[1] ^ k) * BLOCK, BLOCK)
        outs[k][...] = total[pl.ds(at, BLOCK), :].astype(outs[k].dtype)


BLOCK_OUTS = [(shape(BLOCK, D, dtype=f32), VMEM)] + [(shape(BLOCK, D), VMEM)] * 3


def out_kernel(info, mine, got, *refs):
    pieces, outs, (weight, total, sem) = refs[:8], refs[8:12], refs[12:]
    core = info[0]
    load_pieces(info.at[pl.ds(8, 64)], pieces, weight, 768, 256, sem)
    mine, got = mine.get(), got.get()
    wait_all(weight, sem)
    own = core == 0
    left = [jnp.where(own, mine[0], got[0]), jnp.where(own, got[0], mine[0])]
    total[...] = dot_nn(jnp.concatenate(left, axis=1), weight[...].reshape(512, D))
    write_blocks(info, total, outs)


def project_out(info, mine, got, pieces, after=()):
    return call(
        out_kernel,
        [SMEM] + [LOAD] * 2 + [ANY] * 8,
        BLOCK_OUTS,
        [pltpu.VMEM((2, 256, D), bf16), TOTAL, pltpu.SemaphoreType.DMA],
        [info, mine, got, *pieces],
        limit=20,
        cost=1000,
        after=after,
    )


def out_back_kernel(info, *refs):
    acts, pieces = refs[:4], refs[4:12]
    keep, away, weight, act, sems = refs[12:]
    core = info[0]
    fetch(info, acts, act, sems.at[0])
    load_pieces(info.at[pl.ds(8, 64)], pieces, weight, 768, 256, sems.at[1])
    wait_all(act, sems.at[0])
    wait_all(weight, sems.at[1])
    for which, out in ((1, away), (0, keep)):
        out.ref[0] = dot_nt(act[...], weight[core ^ which]).astype(bf16)
        out.send()


def project_out_back(info, acts, pieces, after=()):
    return call(
        out_back_kernel,
        [SMEM] + [ANY] * 12,
        [(shape(1, 512, WIDTH), STORE)] * 2,
        [pltpu.VMEM((2, 256, D), bf16), ROWS, pltpu.SemaphoreType.DMA((2,))],
        [info, *acts, *pieces],
        after=after,
    )


def qkv_back_kernel(info, mine, got, *refs):
    pieces, acts = refs[:8], refs[8:12]
    out, gain, weight, total, act, sem, act_sem = refs[12:]
    fetch(info, acts, act, act_sem)
    core = info[0]
    load_pieces(info.at[pl.ds(8, 64)], pieces, weight, 0, 768, sem)
    wait_all(weight, sem)
    mine, got = mine.get(), got.get()
    own = core == 0
    left = [jnp.where(own, mine[m], got[m]) for m in range(3)]
    left += [jnp.where(own, got[m], mine[m]) for m in range(3)]
    total[...] = dot_nn(jnp.concatenate(left, axis=1), weight[...].reshape(1536, D))
    out.ref[...] = total[...].astype(bf16)
    out.send()
    wait_all(act, act_sem)
    gain[...] = jnp.sum(total[...] * act[...].astype(f32), axis=0, keepdims=True)


def project_qkv_back(info, mine, got, pieces, acts, after=()):
    return call(
        qkv_back_kernel,
        [SMEM] + [LOAD] * 2 + [ANY] * 12,
        [(shape(512, D), STORE), (shape(1, D, dtype=f32), VMEM)],
        [pltpu.VMEM((2, 768, D), bf16), TOTAL, ROWS]
        + [pltpu.SemaphoreType.DMA] * 2,
        [info, mine, got, *pieces, *acts],
        after=after,
    )


def load_gathered(weights, target, s, first, rows, row, sem):
    for x in range(4):
        for y in range(2):
            for c in range(2):
                f = x * 4 + y * 2 + c
                pltpu.make_async_copy(
                    weights.at[x * 8 + y * 4 + s * 2 + c, pl.ds(first, rows), :],
                    target.at[s, pl.ds(row, rows), f * 128 : f * 128 + 128],
                    sem,
                ).start()


def mlp_kernel(info, *refs):
    acts, cots, weights = refs[:4], refs[4:8], refs[8]
    hid, gate_grad, up_grad = refs[9:12]
    outs = refs[12:16]
    weight, act, cot, total, both, sems = refs[16:]
    n = UNITS
    fetch(info, acts, act, sems.at[3])
    load_gathered(weights, weight, 0, 0, n, 0, sems.at[0])
    load_gathered(weights, weight, 0, n, 2 * n, n, sems.at[1])
    fetch(info, cots, cot, sems.at[4])
    wait_all(act, sems.at[3])
    for s in range(2):
        if s == 0:
            wait_all(weight.at[0, pl.ds(0, n), :], sems.at[0])
        else:
            wait_all(weight.at[1], sems.at[2])
        gate = dot_nt(act[...], weight[s, pl.ds(0, n), :])
        if s == 0:
            load_gathered(weights, weight, 1, 0, 3 * n, 0, sems.at[2])
            wait_all(weight.at[0, pl.ds(n, 2 * n), :], sems.at[1])
            wait_all(cot, sems.at[4])
        up = dot_nt(act[...], weight[s, pl.ds(n, n), :])
        hg = dot_nt(cot[...], weight[s, pl.ds(2 * n, n), :])
        sig = 1.0 / (1.0 + jnp.exp(-gate))
        silu = gate * sig
        hid.ref[s] = (silu * up).astype(bf16)
        gate_grad.ref[s] = (hg * up * (sig * (1.0 + gate * (1.0 - sig)))).astype(bf16)
        up_grad.ref[s] = (hg * silu).astype(bf16)
        for result in (hid, gate_grad, up_grad):
            result.send(s)
        both[:, 0:n] = gate_grad.ref[s]
        both[:, n : 2 * n] = up_grad.ref[s]
        part = dot_nn(both[...], weight[s, pl.ds(0, 2 * n), :])
        if s == 0:
            total[...] = part
        else:
            total[...] += part
    for k in (2, 1, 3, 0):
        at = pl.multiple_of((info[1] ^ k) * BLOCK, BLOCK)
        outs[k].ref[...] = total[pl.ds(at, BLOCK), :].astype(outs[k].ref.dtype)
        outs[k].send()


def mlp(info, acts, cots, weights, after=()):
    return call(
        mlp_kernel,
        [SMEM] + [ANY] * 9,
        [(shape(2, 512, UNITS), STORE)] * 3
        + [(shape(BLOCK, D, dtype=f32), STORE)]
        + [(shape(BLOCK, D), STORE)] * 3,
        [
            pltpu.VMEM((2, 3 * UNITS, D), bf16), ROWS, ROWS, TOTAL,
            pltpu.VMEM((512, 2 * UNITS), bf16), pltpu.SemaphoreType.DMA((5,)),
        ],
        [info, *acts, *cots, weights],
        after=after,
    )


def down_kernel(hid, weights, out, weight, total, sems):
    for s in range(2):
        load_gathered(weights, weight, s, 2 * UNITS, UNITS, 0, sems.at[s])
    hid = hid.get()
    wait_all(weight.at[0], sems.at[0])
    total[...] = dot_nn(hid[0], weight[0])
    wait_all(weight.at[1], sems.at[1])
    out.ref[...] = (total[...] + dot_nn(hid[1], weight[1])).astype(bf16)
    out.send()


def project_down(hid, weights, after=()):
    return call(
        down_kernel,
        [LOAD, ANY],
        [(shape(512, D), STORE)],
        [pltpu.VMEM((2, UNITS, D), bf16), TOTAL, pltpu.SemaphoreType.DMA((2,))],
        [hid, weights],
        after=after,
    )


def half_features(info, source, target, which):
    core, x, y = info[0], info[2], info[3]
    for dx in range(4):
        for dlo in range(2):
            lane = ((x ^ dx) * 4 + (y ^ dlo) * 2 + (core ^ which)) * 128
            b = 2 * dx + dlo
            target[:, 128 * b : 128 * b + 128] = source[:, pl.ds(pl.multiple_of(lane, 128), 128)]


class Joined:
    def __init__(self, ref):
        self.ref = ref

    def __getitem__(self, j):
        return self.ref.at[j]


def send_blocks(on_core, stage, slot, outs, rows, count, h, sem):
    def send(c):
        for dx in range(4):
            for dlo in range(2):
                dy = dlo + 2 * h
                i, j = (dx, dy) if c == 0 else (dy, dx)
                pltpu.make_async_copy(
                    stage.at[slot, 2 * dx + dlo, pl.ds(0, count), :],
                    outs[j].at[i, rows, :],
                    sem,
                ).start()

    pl.when(on_core == 0)(functools.partial(send, 0))
    pl.when(on_core == 1)(functools.partial(send, 1))


def half_grads(on_core, lefts, rights, spans, outs, stage, sems, got=None):
    step = 0
    for m, (first, count) in enumerate(spans):
        right = rights[m]()
        rows = pl.ds(first, count)
        for h in range(2):
            slot = step % 2
            part = dot_tn(lefts(h, m), right[...])
            if step >= 2:
                before = pl.ds(0, spans[(step - 2) // 2][1])
                wait_all(stage.at[slot, :, before, :], sems.at[slot])
            more = got(m) if got else None
            for dx in range(4):
                for dlo in range(2):
                    b, dy = 2 * dx + dlo, dlo + 2 * h
                    block = part[:, 128 * b : 128 * b + 128]
                    if got:
                        i = jnp.where(on_core == 0, dx, dy)
                        j = jnp.where(on_core == 0, dy, dx)
                        block = block + more[j, i, rows, :].astype(f32)
                    stage[slot, b, 0:count, :] = block.astype(bf16)
            send_blocks(on_core, stage, slot, outs, rows, count, h, sems.at[slot])
            step += 1
    for slot in range(2):
        wait_all(stage.at[slot, :, pl.ds(0, spans[-1][1]), :], sems.at[slot])


def load_got(pieces, target, spans, sems):
    for m, (first, count) in enumerate(spans):
        rows = pl.ds(first, count)
        for j in range(4):
            pltpu.make_async_copy(
                pieces[j].at[:, rows, :], target.at[j, :, rows, :], sems.at[m]
            ).start()
    waited = []

    def got(m):
        if m not in waited:
            waited.append(m)
            part = target.at[:, :, pl.ds(*spans[m]), :]
            pltpu.make_async_copy(part, part, sems.at[m]).wait()
        return target

    return got


MLP_SPANS = [(0, UNITS), (UNITS, UNITS), (2 * UNITS, UNITS)]
ATTN_SPANS = [(0, 3 * WIDTH), (3 * WIDTH, WIDTH)]


def mlp_rights(info, acts, cots, act, cot, act_half, cot_half, sems, which):
    fetch(info, acts, act, sems.at[0])
    fetch(info, cots, cot, sems.at[1])

    def first():
        wait_all(act, sems.at[0])
        half_features(info, act, act_half, which)
        return act_half

    def last():
        wait_all(cot, sems.at[1])
        half_features(info, cot, cot_half, which)
        return cot_half

    return first, lambda: act_half, last


def mlp_grads_kernel(which, info, gate_grad, up_grad, hid, *refs):
    acts, cots, refs = refs[:4], refs[4:8], refs[8:]
    got = None
    if which == 0:
        piece, outs, refs = Joined(refs[0]), refs[2:6], refs[7:]
    else:
        outs, refs = Joined(refs[0]), refs[1:]
    act, cot, act_half, cot_half, stage, sems, in_sems = refs[:7]
    rights = mlp_rights(info, acts, cots, act, cot, act_half, cot_half, in_sems, which)
    if which == 0:
        got = load_got(piece, refs[7], MLP_SPANS, refs[8])
    sources = (gate_grad, up_grad, hid)
    half_grads(
        info[0] ^ which, lambda h, m: sources[m].get()[info[4] ^ h], rights, MLP_SPANS, outs,
        stage, sems, got,
    )


def mlp_grads(which, info, hid, gate_grad, up_grad, acts, cots, got=(), passed=(), after=()):
    scratch = [
        ROWS, ROWS, HALF, HALF, pltpu.VMEM((2, 8, UNITS, 128), bf16),
        pltpu.SemaphoreType.DMA((2,)), pltpu.SemaphoreType.DMA((2,)),
    ]
    if which == 0:
        scratch += [pltpu.VMEM((4, 4, 3 * UNITS, 128), bf16), pltpu.SemaphoreType.DMA((3,))]
    return call(
        functools.partial(mlp_grads_kernel, which),
        [SMEM] + [LOAD] * 3 + [ANY] * (8 + len(got) + len(passed)),
        [(shape(4, 3 * UNITS, 128), ANY)] * 4 + [(shape(*v.shape), ANY) for v in passed]
        if which == 0 else [(shape(4, 4, 3 * UNITS, 128), ANY)],
        scratch,
        [info, gate_grad, up_grad, hid, *acts, *cots, *got, *passed],
        after=after,
        aliases={13: 4} if passed else None,
    )


def split_gains(gains, total, halves):
    for b in range(16):
        lanes = slice(128 * b, 128 * b + 128)
        total[b : b + 1, :] = gains[0:1, lanes]
        total[16 + b : 17 + b, :] = gains[1:2, lanes]
    coarse = total[...].astype(bf16)
    halves[0:32, :] = coarse
    halves[32:64, :] = (total[...] - coarse.astype(f32)).astype(bf16)


def attn_grads_kernel(which, info, mine, got_heads, att_mine, att_got, *refs):
    mids, acts, refs = refs[:4], refs[4:8], refs[8:]
    got = None
    if which == 0:
        piece, gains, outs, refs = Joined(refs[0]), refs[1], refs[2:6], refs[6:]
        split_gains(gains, *refs[10:12])
        for j in range(4):
            for i in range(4):
                pltpu.make_async_copy(
                    refs[11].at[pl.ds(16 * i, 16), :],
                    outs[j].at[i, pl.ds(4 * WIDTH, 16), :],
                    refs[12],
                ).start()
    else:
        outs, refs = Joined(refs[0]), refs[1:]
    left, act_half, mid_half, stage, sems, act, mid, in_sems = refs[:8]
    fetch(info, acts, act, in_sems.at[0])
    fetch(info, mids, mid, in_sems.at[1])
    if which == 0:
        got = load_got(piece, refs[8], ATTN_SPANS, refs[9])
    for w, (grads, att) in enumerate(((mine, att_mine), (got_heads, att_got))):
        for m in range(3):
            left[w, :, WIDTH * m : WIDTH * m + WIDTH] = grads.get()[m]
        left[w, :, 3 * WIDTH :] = att.get()[0]

    def first():
        wait_all(act, in_sems.at[0])
        half_features(info, act, act_half, which)
        return act_half

    def last():
        wait_all(mid, in_sems.at[1])
        half_features(info, mid, mid_half, which)
        return mid_half

    half_grads(
        info[0] ^ which,
        lambda h, m: left[
            info[0] ^ info[4] ^ h, :, ATTN_SPANS[m][0] : sum(ATTN_SPANS[m])
        ],
        (first, last), ATTN_SPANS, outs, stage, sems, got,
    )
    if which == 0:
        for j in range(4):
            wait_all(refs[11], refs[12])


def attn_grads(which, info, operands, got=(), gains=(), after=()):
    scratch = [
        pltpu.VMEM((2, 512, 4 * WIDTH), bf16), HALF, HALF,
        pltpu.VMEM((2, 8, 3 * WIDTH, 128), bf16), pltpu.SemaphoreType.DMA((2,)),
        ROWS, ROWS, pltpu.SemaphoreType.DMA((2,)),
    ]
    if which == 0:
        scratch += [
            pltpu.VMEM((4, 4, 4 * WIDTH, 128), bf16), pltpu.SemaphoreType.DMA((2,)),
            pltpu.VMEM((32, 128), f32), pltpu.VMEM((64, 128), bf16), pltpu.SemaphoreType.DMA,
        ]
    return call(
        functools.partial(attn_grads_kernel, which),
        [SMEM] + [LOAD] * 4 + [ANY] * (8 + len(got)) + [VMEM] * len(gains),
        [(shape(4, 4 * WIDTH + 16, 128), ANY)] * 4 if which == 0 else
        [(shape(4, 4, 4 * WIDTH, 128), ANY)],
        scratch,
        [info, *operands, *got, *gains],
        after=after,
    )


def norm_back(x, gain, gradient):
    inverse = lax.rsqrt(jnp.mean(x * x, axis=-1, keepdims=True) + epsilon)
    scaled = gradient * gain
    mean_term = jnp.mean(scaled * x, axis=-1, keepdims=True)
    back = inverse * scaled - x * (inverse * inverse * inverse) * mean_term
    return back, inverse


def middle_back_kernel(middle, gain, cotangent, *refs):
    gradient, (out, low, gain_part) = refs[:4], refs[4:]
    x, e = middle[...], gradient[0][...]
    for v in gradient[1:]:
        e = e + v[...].astype(f32)
    back, inverse = norm_back(x, gain[...], e)
    total = cotangent[...].astype(f32) + back
    out[...] = total
    low[...] = total.astype(bf16)
    gain_part[...] = jnp.sum(e * x * inverse, axis=0, keepdims=True)


def middle_back(middle, gain, gradient, cotangent, after):
    return call(
        middle_back_kernel,
        [VMEM] * 7,
        [
            (shape(BLOCK, D, dtype=f32), VMEM),
            (shape(BLOCK, D), VMEM),
            (shape(1, D, dtype=f32), VMEM),
        ],
        [],
        [middle, gain[None], cotangent, *gradient],
        after=after,
    )


def input_back_kernel(stream, gain, gradient, middle, out):
    back, _ = norm_back(stream[0:BLOCK, :].astype(f32), gain[...], gradient[...].astype(f32))
    out[...] = (middle[...] + back).astype(bf16)


def input_back(stream, gain, gradient, middle, after):
    return call(
        input_back_kernel,
        [VMEM] * 4,
        [(shape(BLOCK, D), VMEM)],
        [],
        [stream, gain[None], gradient, middle],
        after=after,
    )[0]


def second_sum(parts, gains=False, after=(), passed=()):
    rows = parts[0].shape[1] - 16 * gains
    more = 64 * gains

    def second_sum_kernel(*refs):
        sources, outs = refs[:4], refs[4 + len(passed) : 8 + len(passed)]
        ins, sems = refs[-2:]
        for k in (1, 2, 3, 0):
            for v in range(4):
                pltpu.make_async_copy(sources[v].at[k], ins.at[k, v], sems.at[k]).start()
        if gains:
            for k in range(4):
                wait_all(ins.at[k], sems.at[k])
            low = pl.ds(rows, 16)
            part = []
            for v in range(4):
                coarse = jnp.concatenate([ins[0, v, low, :], ins[1, v, low, :]], axis=0)
                fine = jnp.concatenate([ins[2, v, low, :], ins[3, v, low, :]], axis=0)
                part.append(coarse.astype(f32) + fine.astype(f32))
            total = (part[0] + part[1]) + (part[2] + part[3])
            coarse = total.astype(bf16)
            fine = (total - coarse.astype(f32)).astype(bf16)
        for k in (1, 2, 3, 0):
            out = outs[k].ref
            if not gains:
                wait_all(ins.at[k], sems.at[k])
            total = ins[k, 0, 0:rows, :].astype(f32)
            for v in range(1, 4):
                total = total + ins[k, v, 0:rows, :].astype(f32)
            out[0:rows, :] = total.astype(out.dtype)
            if gains:
                out[rows : rows + 32, :] = coarse.astype(out.dtype)
                out[rows + 32 :, :] = fine.astype(out.dtype)
            outs[k].send()

    return call(
        second_sum_kernel,
        [ANY] * (4 + len(passed)),
        [(shape(rows + more, 128, dtype=f32 if k == 0 else bf16), STORE) for k in range(4)]
        + [(shape(*v.shape), ANY) for v in passed],
        [pltpu.VMEM((4, 4, *parts[0].shape[1:]), bf16), pltpu.SemaphoreType.DMA((4,))],
        [*parts, *passed],
        after=after,
        aliases={4: 4} if passed else None,
    )


def final_sum(parts, plan, after=()):
    def final_sum_kernel(*refs):
        ins, outs = refs[:4], refs[4:]
        for (first, rows, turn), out in zip(plan, outs):
            part = [v[first : first + rows, :].astype(f32) for v in ins]
            total = (part[0] + part[1]) + (part[2] + part[3])
            out[...] = total.T if turn else total

    outs = [
        (shape(*((128, rows) if turn else (rows, 128)), dtype=f32), VMEM)
        for _, rows, turn in plan
    ]
    return call(final_sum_kernel, [VMEM] * 4, outs, [], list(parts), limit=24, cost=1000, after=after)


def widen_kernel(value, out):
    out[...] = value[...].astype(f32)


def widen(value, after=()):
    return call(
        widen_kernel,
        [VMEM],
        [(shape(*value.shape, dtype=f32), VMEM)],
        [],
        [value],
        after=after,
        cost=1000,
    )[0]


def stack_attn_kernel(query, key, value, output, out):
    w = WIDTH
    for m, ref in enumerate((query, key, value)):
        out[w * m : w * m + w, :] = ref[...].T
    out[3 * w :, :] = output[...]


def stack_attn(query, key, value, output):
    return call(
        stack_attn_kernel,
        [VMEM] * 4,
        [(shape(4 * WIDTH, 128), VMEM)],
        [],
        [query, key, value, output],
        cost=1000,
    )[0]


def joined_kernel(stream, more, out):
    out[...] = (stream[...] + more[...].astype(f32)).astype(bf16)


def joined(stream, more, after):
    return call(
        joined_kernel,
        [VMEM] * 2,
        [(shape(BLOCK, D), VMEM)],
        [],
        [stream, more],
        after=after,
        cost=1000,
    )[0]


def stack_kernel(*refs):
    gate, up, down, out = refs[0], refs[1], refs[2], refs[-1]
    out[0:UNITS, :] = gate[...]
    out[UNITS : 2 * UNITS, :] = up[...]
    out[2 * UNITS :, :] = down[...]


def stack_mlp(gate, up, down, after=()):
    return call(
        stack_kernel,
        [VMEM] * 3,
        [(shape(3 * UNITS, 128), VMEM)],
        [],
        [gate, up, down],
        after=after,
    )[0]


def copy_kernel(value, out):
    out[...] = value[...]


def copied(value, after):
    return call(copy_kernel, [VMEM], [(shape(*value.shape, dtype=value.dtype), VMEM)], [], [value], after=after)[0]


def held_kernel(*refs):
    del refs


def held_all(values, after):
    return call(
        held_kernel,
        [ANY] * len(values),
        [(shape(*v.shape, dtype=v.dtype), ANY) for v in values],
        [],
        values,
        after=after,
        aliases={k: k for k in range(len(values))},
        cost=1000,
    )


def held(value, after):
    return held_all([value], after)[0]


def row_kernel(*refs):
    parts, row, twin = refs[:4], refs[4], refs[5]
    copies = []
    for k in range(4):
        row.ref[k] = parts[k].get()[...]
        row.send(k)
        copies.append(pltpu.make_async_copy(row.ref.at[k], twin.at[k], refs[6].at[k]))
        copies[-1].start()
    for copy in copies:
        copy.wait()


def joined_row(parts):
    out = shape(4, *parts[0].shape)
    return call(
        row_kernel,
        [LOAD] * 4,
        [(out, STORE), (out, ANY)],
        [pltpu.SemaphoreType.DMA((4,))],
        parts,
        cost=1000,
    )


def norm_kernel(stream, gain, out):
    x = stream[0:BLOCK, :].astype(f32)
    inverse = lax.rsqrt(jnp.mean(x * x, axis=-1, keepdims=True) + epsilon)
    out[...] = (x * inverse * gain[...]).astype(bf16)


def normed(stream, gain, after):
    return call(
        norm_kernel,
        [VMEM] * 2,
        [(shape(BLOCK, D), VMEM)],
        [],
        [stream, gain[None]],
        after=after,
    )[0]


def swap_bits(value, axes, change, name):
    sizes = [SIZES[a] for a in axes]
    pairs = []
    for index in np.ndindex(*sizes):
        pairs.append(
            (
                int(np.ravel_multi_index(index, sizes)),
                int(np.ravel_multi_index(change(*index), sizes)),
            )
        )
    with jax.named_scope(name):
        return lax.ppermute(value, axes if len(axes) > 1 else axes[0], pairs)


def over_z(value, k):
    return swap_bits(value, ("z",), lambda z: (z ^ k,), f"over_z{k}")


def over_x(value, k):
    return swap_bits(value, ("x",), lambda x: (x ^ k,), f"over_x{k}")


def over_y(value, k):
    return swap_bits(value, ("ylo", "yhi"), lambda lo, hi: (lo ^ (k & 1), hi ^ (k >> 1)), f"over_y{k}")


def over_core(value):
    return swap_bits(value, ("core",), lambda c: (c ^ 1,), "over_core")


def exchange(value):
    return swap_bits(value, ("core", "yhi"), lambda c, h: (h, c), "exchange")


def across(value, k, first):
    def change(x, lo, core, hi):
        if (core == 0) == first:
            return (x ^ k, lo, core, hi)
        return (x, lo ^ (k & 1), core, hi ^ (k >> 1))

    return swap_bits(value, ("x", "ylo", "core", "yhi"), change, f"across{k}" if first else f"second{k}")


def second_step(parts):
    return [parts[0]] + [across(parts[k], k, False) for k in (1, 2, 3)]


def first_step(parts):
    out = parts[0]
    for k in (1, 2, 3):
        out = out + across(parts[k], k, True).astype(f32)
    return out


def gather_tokens(value):
    return [value] + [over_z(value, k) for k in (1, 2, 3)]


def scatter_tokens(blocks):
    out = blocks[0]
    for k in (1, 2, 3):
        out = out + over_z(blocks[k], k).astype(f32)
    return out


def norm_forward(stream, gain):
    inverse = lax.rsqrt(jnp.mean(stream * stream, axis=-1, keepdims=True) + epsilon)
    return (stream * inverse * gain).astype(bf16), inverse


def body(
    block_input,
    segments,
    positions,
    attn_gain,
    w_query,
    w_key,
    w_value,
    w_output,
    mlp_gain,
    w_gate,
    w_up,
    w_down,
    cotangent,
):
    at_x, at_ylo, at_core, at_yhi, at_z = (lax.axis_index(a).astype(jnp.int32) for a in AXES)

    place = []
    for other in range(2):
        source = at_core ^ other
        for j in range(4):
            for i in range(4):
                dx = jnp.where(source == 0, i, j)
                dy = jnp.where(source == 0, j, i)
                place.append(at_yhi ^ (dy >> 1))
                place.append((at_x ^ dx) * 4 + (at_ylo ^ (dy & 1)) * 2 + source)
    zero = jnp.zeros((), jnp.int32)
    info = jnp.stack([at_core, at_z, at_x, at_ylo, at_yhi, zero, zero, zero] + place)

    extra = jnp.stack(
        [
            jnp.concatenate([positions // 64, positions % 64]),
            jnp.concatenate([segments, jnp.zeros_like(segments)]),
        ]
    ).astype(bf16)
    low_input = exchange(
        jnp.concatenate([block_input.astype(bf16), jnp.pad(extra, ((0, 14), (0, 0)))])
    )
    extra = low_input[BLOCK : BLOCK + 2].astype(f32)
    pos = extra[0, :1024] * 64.0 + extra[0, 1024:]
    segs = extra[1, :1024].astype(jnp.int32)
    seg_col, seg_row = segs[:, None], segs[None, :]
    frequency = base_freq ** (-(2.0 * jnp.arange(HEAD_DIM // 2, dtype=f32)) / HEAD_DIM)
    angles = pos[:, None] * frequency[None, :]
    cosine, sine = jnp.cos(angles), jnp.sin(angles)
    cosine = jnp.concatenate([cosine, cosine], axis=1)
    sine = jnp.concatenate([-sine, sine], axis=1)

    piece = stack_attn(w_query, w_key, w_value, w_output)
    grad_low = cotangent.astype(bf16)
    parts = [piece] + [across(piece, k, True) for k in (1, 2, 3)]
    row, twin = joined_row(parts)
    grad_low = held(grad_low, [row])
    act1 = normed(low_input, attn_gain, [row, grad_low])
    grad_low = exchange(grad_low)
    act1_all = gather_tokens(act1)
    pieces = [row, across(row, 1, False), None, across(row, 3, False)]
    pieces[2] = across(held(twin, [pieces[1], pieces[3], act1]), 2, False)
    pieces = pieces + [over_core(v) for v in pieces]
    cot_all = gather_tokens(grad_low)
    def own_rows(table):
        return lax.dynamic_slice_in_dim(table, at_core * 512, 512, axis=0)

    tables = [own_rows(cosine), own_rows(sine)]
    piece_mlp = stack_mlp(w_gate.T, w_up.T, w_down, after=[cosine, sine, seg_col, *tables])
    piece_mlp = held(piece_mlp, [*pieces[1:4], *act1_all[1:], grad_low])
    weights_mlp = lax.all_gather(piece_mlp, ("x", "ylo", "yhi", "core"))

    keep, *away = project_qkv(info, act1_all, pieces, *tables, after=[piece_mlp])
    qkv_mine, qkv_got = keep, [over_core(v) for v in away]
    keep, away = attend(info, qkv_mine, qkv_got, seg_col, seg_row, after=[cot_all[1], cot_all[3]])
    att_mine, att_got = keep, over_core(away)
    blocks = project_out(info, att_mine, att_got, pieces, after=cot_all[2:3])
    stream = low_input[:BLOCK].astype(f32)
    inverse1 = lax.rsqrt(jnp.mean(stream * stream, axis=-1, keepdims=True) + epsilon)
    middle = stream + scatter_tokens(blocks)
    act2, inverse2 = norm_forward(middle, mlp_gain)
    act2_all = gather_tokens(act2)

    hid, gate_grad, up_grad, *blocks = mlp(info, act2_all, cot_all, weights_mlp)
    grad_act2 = [blocks[0]] + [over_z(blocks[k], k) for k in (1, 2, 3)]
    operands = [info, hid, gate_grad, up_grad, act2_all, cot_all]
    (away,) = mlp_grads(1, *operands)
    got = over_core(away)
    (down,) = project_down(hid, weights_mlp, after=[away])
    grad_middle, middle_low, gain2_part = middle_back(
        middle, mlp_gain, grad_act2, grad_low, [down, got]
    )
    mid_all = gather_tokens(middle_low)
    *parts, down = mlp_grads(0, *operands, [got], [down], after=[middle_low])
    first, third = across(parts[1], 1, False), across(parts[3], 3, False)
    keep, away = project_out_back(info, mid_all, pieces, after=parts[:1])
    down = lax.psum_scatter(down, "z", tiled=True)
    keep, away = attend_back(
        info, qkv_mine, qkv_got, keep, over_core(away), seg_col, seg_row, cosine, sine
    )
    kept = held(parts[2], [keep, first, third])
    parts = [parts[0], first, across(kept, 2, False), third]
    g_mine, g_got = keep, over_core(away)
    operands = [g_mine, g_got, att_mine, att_got, *mid_all, *act1_all]
    (away,) = attn_grads(1, info, operands, after=[kept])
    got = over_core(away)
    partial, gain1_part = project_qkv_back(info, g_mine, g_got, pieces, act1_all, after=[away])
    parts = second_sum(parts, after=[gain1_part])
    out_block = exchange(joined(middle, down, parts[:1]))
    grad_act1 = lax.psum_scatter(partial, "z", tiled=True)
    parts = [parts[0]] + [across(parts[k], k, True) for k in (1, 2, 3)]
    gains = [jnp.concatenate([gain1_part / attn_gain, gain2_part])]
    outs = attn_grads(0, info, operands, [got], gains, after=parts[:1])
    grad_input = input_back(
        low_input, attn_gain, grad_act1, grad_middle, [outs[0]]
    )
    grad_gate, grad_up, grad_down = final_sum(
        parts, ((0, UNITS, False), (UNITS, UNITS, False), (2 * UNITS, UNITS, False)), [grad_input]
    )
    out_block = widen(out_block, [grad_input])
    *parts, grad_input = second_sum(
        second_step(outs), True, [grad_down, out_block], [grad_input]
    )
    grad_input = widen(exchange(grad_input))
    parts = [parts[0]] + [across(parts[k], k, True) for k in (1, 2, 3)]
    w, n = WIDTH, UNITS
    grad_query, grad_key, grad_value, grad_output, coarse, fine = final_sum(
        parts,
        ((0, w, True), (w, w, True), (2 * w, w, True), (3 * w, w, False),
         (4 * w, 32, False), (4 * w + 32, 32, False)),
        [grad_input],
    )
    gains = (coarse + fine).reshape(2, D)
    one, two, three = (over_z(gains, k) for k in (1, 2, 3))
    gains = (gains + one) + (two + three)
    gains = gains + over_core(gains)
    return (
        out_block,
        grad_input,
        gains[0],
        grad_query,
        grad_key,
        grad_value,
        grad_output,
        gains[1],
        grad_gate.T,
        grad_up.T,
        grad_down,
    )


def solution(mesh):
    inner = Mesh(np.asarray(mesh.devices).reshape([SIZES[a] for a in AXES]), AXES)
    dp, tensor = ("x", "ylo", "core"), ("yhi", "z")
    rows, wide, tall = P(dp + tensor, None), P(dp, tensor), P(tensor, dp)
    return jax.shard_map(
        body,
        mesh=inner,
        in_specs=(
            rows, P(dp), P(dp), P(), wide, wide, wide, tall, P(), wide, wide, tall, rows,
        ),
        out_specs=(rows, rows, P(), wide, wide, wide, tall, P(), wide, wide, tall),
        check_vma=False,
    )
```
